32 devices in a mesh: grid: 4 (over z), dom: 8 (over y, x, core).
Axes of the slice: x: 2, y: 2, z: 4, core: 2. Of those that a mesh axis runs over, the one named last changes fastest.
Arguments:
- nodal_values: float32 [8, 256, 8192], P('grid', None, 'dom'), may hold values from -6 to 6
- source_term: float32 [8, 256, 8192], P('grid', None, 'dom'), may hold values from -6 to 6
- velocity: float32 [8, 2], P('grid'), may hold values from 0.2 to 0.9
- react_rate: float32 [8], P('grid'), may hold values from 0.3 to 3
- levels: int32 [8, 2], P('grid'), may hold values from 5 to 8, as said below
- comb_coefs: int32 [8], P('grid'), may hold values from -1 to 1, as said below
Outputs:
- combined: float32 [8, 256, 8192], P('grid', None, 'dom')
The draws below stay inside these ranges and needn't reach their ends.
Inputs may be any that keep to these rules, and one draw needn't show every extreme that they name: Each grid's two levels sum to 13 or 12. comb_coefs[c] is 1 where the levels of grid c sum to 13 and -1 where they sum to 12.
All inputs are finite; a program needn't handle non-finite values.
Results may differ from the reference program's by a relative error of at most 0.0003.
Values sent between devices are 32-bit elements; how exact they have to be, the bound alone decides.
No kernel may reach another device: no remote copies, remote signals or barrier semaphores. Data moves between devices by JAX's collectives and lax.ppermute only.
A program may use at most 64 MiB of HBM per device.

```python
import math
import jax
import jax.numpy as jnp
from jax import lax

MAXL = 8
LINE = 256
LSUM = 13
MINL = 5
CELLS = 8192
COMP = 8
R = 256
N_DOM = 8


def pick_levels(key):
    inner_key = jax.random.fold_in(key, 7)
    first_key, second_key = jax.random.split(inner_key)
    lower_sum = jax.random.randint(first_key, (COMP,), 0, 2)
    level_cols = MINL + jax.random.randint(second_key, (COMP,), 0, 4 - lower_sum)
    level_rows = LSUM - lower_sum - level_cols
    return (lower_sum, level_cols, level_rows)


def draw_levels(key, part):
    lower_sum, level_cols, level_rows = pick_levels(key)
    return jnp.stack([level_cols, level_rows], axis=-1).astype(jnp.int32)


def draw_comb_coefs(key, part):
    lower_sum, level_cols, level_rows = pick_levels(key)
    return (1 - 2 * lower_sum).astype(jnp.int32)


def level_of(key, extent, cuts, smallest, high):
    gain = 1.0
    for dim, blocks in cuts:
        heights = jax.random.uniform(jax.random.fold_in(jax.random.fold_in(key, 6), dim), (blocks,), jnp.float32, smallest / len(cuts), high / len(cuts))
        gain = gain * jnp.repeat(jnp.exp(heights), extent[dim] // blocks).reshape((-1,) + (1,) * (len(extent) - 1 - dim))
    return gain


def bell_draw(key, extent, scale, limit, cuts=(), held_as=jnp.bfloat16):
    loudness = level_of(key, extent, cuts, -0.22, 0.18) if cuts else 1.0
    drawn = jax.random.normal(key, extent, jnp.float32) * scale * loudness
    return jnp.minimum(jnp.maximum(drawn, -limit), limit).astype(held_as)


def setup_inputs(seed: int = 0) -> dict:
    key_list = jax.random.split(jax.random.key(seed), 7)
    return {
        "nodal_values": bell_draw(key_list[0], (COMP, R, CELLS), 1.0, 6.0, ((0, 4), (2, 8)), jnp.float32),
        "source_term": bell_draw(key_list[1], (COMP, R, CELLS), 1.0, 6.0, ((0, 4), (2, 8)), jnp.float32),
        "velocity": jnp.clip(0.2 + 0.7 * jax.random.uniform(key_list[2], (COMP, 2), jnp.float32) ** level_of(key_list[2], (COMP, 2), ((0, 4),), -0.2, 0.2), 0.2, 0.9),
        "react_rate": jnp.clip(jnp.exp(math.log(3.0) - 2.3025851 * jax.random.uniform(key_list[3], (COMP,), jnp.float32) ** level_of(key_list[3], (COMP,), ((0, 4),), -0.2, 0.2)), 0.3, 3.0),
        "levels": draw_levels(jax.random.fold_in(key_list[6], 71), 0),
        "comb_coefs": draw_comb_coefs(jax.random.fold_in(key_list[6], 71), 0),
    }


tau_react = 0.25


def advect_pair(values, ahead, behind, courant):
    return values - 0.5 * courant * (ahead - behind) + 0.5 * courant * courant * (ahead - 2.0 * values + behind)


def grid_layout(level_pair):
    col_count = jnp.left_shift(jnp.int32(1), level_pair[0])
    row_count = jnp.left_shift(jnp.int32(1), level_pair[1])
    block_len = CELLS // N_DOM
    live_count = col_count * row_count // N_DOM
    rows_block = live_count // col_count
    logical = jnp.arange(CELLS, dtype=jnp.int32)
    in_grid = logical < col_count * row_count
    row_num = jnp.where(in_grid, logical // col_count, 0)
    col_num = jnp.where(in_grid, logical % col_count, 0)
    stored_at = (row_num // rows_block) * block_len + (row_num % rows_block) * col_count + col_num
    slot_dev = logical // block_len
    slot_pos = logical % block_len
    slot_live = slot_pos < live_count
    logical_of = jnp.where(slot_live, (slot_dev * rows_block + slot_pos // col_count) * col_count + slot_pos % col_count, 0)
    fine_at = jnp.left_shift(row_num, MAXL - level_pair[1]) * LINE + jnp.left_shift(col_num, MAXL - level_pair[0])
    return {"cols": col_count, "rows": row_count, "inside": in_grid, "rownum": row_num, "colnum": col_num,
            "stored": stored_at, "slotlive": slot_live, "logical": logical_of, "fine": fine_at}


def neighbour(values, position, line_len, offset, compose):
    return jnp.take(values, compose((position + offset + line_len) % line_len), axis=1)


def hierarchize(values, position, line_len, compose):
    spacing = jnp.bitwise_and(position, -position)
    half_w = jnp.where(position > 0, 0.5, 0.0)
    return values - half_w * (neighbour(values, position, line_len, -spacing, compose) + neighbour(values, position, line_len, spacing, compose))


def dehierarchize(values, position, line_len, compose):
    for exponent in range(MAXL - 1, -1, -1):
        spacing = 2 ** exponent
        enabled_flags = jnp.bitwise_and(position, 2 * spacing - 1) == spacing
        lifted = values + 0.5 * (neighbour(values, position, line_len, -spacing, compose) + neighbour(values, position, line_len, spacing, compose))
        values = jnp.where(enabled_flags, lifted, values)
    return values


def advect_along(values, position, line_len, compose, courant):
    return advect_pair(values, neighbour(values, position, line_len, 1, compose), neighbour(values, position, line_len, -1, compose), courant)


def reference(nodal_values, source_term, velocity, react_rate, levels, comb_coefs):
    def first_phase(grid_items):
        grid_vals, grid_src, grid_vel, grid_rate, level_pair = grid_items
        layout = grid_layout(level_pair)
        col_count = layout["cols"]
        row_count = layout["rows"]
        row_num = layout["rownum"]
        col_num = layout["colnum"]
        by_cols = lambda new_pos: row_num * col_count + new_pos
        by_rows = lambda new_pos: new_pos * col_count + col_num
        inside = layout["inside"].astype(jnp.float32)
        values_now = jnp.take(grid_vals, layout["stored"], axis=1) * inside
        forcing = jnp.take(grid_src, layout["stored"], axis=1) * inside
        nu_cols = grid_vel[0] * col_count.astype(jnp.float32) / LINE
        nu_rows = grid_vel[1] * row_count.astype(jnp.float32) / LINE
        values_now = advect_along(values_now, col_num, col_count, by_cols, nu_cols)
        values_now = values_now * (1.0 - tau_react * grid_rate) + tau_react * forcing
        values_now = advect_along(values_now, row_num, row_count, by_rows, nu_rows)
        values_now = hierarchize(values_now, col_num, col_count, by_cols)
        values_now = hierarchize(values_now, row_num, row_count, by_rows)
        return values_now * inside

    surplus_values = lax.map(first_phase, (nodal_values, source_term, velocity, react_rate, levels))

    def add_grid(running, grid_items):
        surplus, level_pair, weight = grid_items
        layout = grid_layout(level_pair)
        running = running.at[:, layout["fine"]].add(weight.astype(jnp.float32) * surplus)
        return running, None

    total_sum, unused = lax.scan(add_grid, jnp.zeros((R, LINE * LINE), jnp.float32), (surplus_values, levels, comb_coefs))

    def second_phase(grid_items):
        grid_vel, level_pair = grid_items
        layout = grid_layout(level_pair)
        col_count = layout["cols"]
        row_count = layout["rows"]
        row_num = layout["rownum"]
        col_num = layout["colnum"]
        by_cols = lambda new_pos: row_num * col_count + new_pos
        by_rows = lambda new_pos: new_pos * col_count + col_num
        inside = layout["inside"].astype(jnp.float32)
        nu_rows = grid_vel[1] * row_count.astype(jnp.float32) / LINE
        values_now = jnp.take(total_sum, layout["fine"], axis=1) * inside
        values_now = dehierarchize(values_now, row_num, row_count, by_rows)
        values_now = advect_along(values_now, row_num, row_count, by_rows, nu_rows)
        values_now = dehierarchize(values_now, col_num, col_count, by_cols)
        values_now = values_now * inside
        return jnp.take(values_now, layout["logical"], axis=1) * layout["slotlive"].astype(jnp.float32)

    return lax.map(second_phase, (velocity, levels))
```

```python
import functools

import jax
import jax.numpy as jnp
import numpy as np
from jax import lax
from jax.experimental import pallas as pl
from jax.experimental.pallas import tpu as pltpu
from jax.sharding import PartitionSpec as P

MAXL = 8
MINL = 5
LSUM = 13
LINE = 2**MAXL
BASE = 2**MINL
TAU = 0.25
VMEM_BYTES = 48 * 2**20
EXACT = lax.Precision.HIGHEST

GROUPS = [(b, y) for b in range(MINL, MAXL + 1) for y in range(MINL, LSUM - b + 1)]
BAND_UNITS = [1] + [2**t for t in range(MAXL - MINL)]
BAND_FIRST = [0] + [2**t for t in range(MAXL - MINL)]


def group_rows(y):
    return 1 if y == MINL else 2 ** (y - MINL - 1)


GROUP_UNITS = [group_rows(y) * BAND_UNITS[b - MINL] for b, y in GROUPS]
TOTAL_UNITS = sum(GROUP_UNITS)
GROUP_OF = [[GROUPS.index((b, y)) if (b, y) in GROUPS else 0 for y in range(MINL, MAXL + 1)] for b in range(MINL, MAXL + 1)]
HEAD_GROUPS = [k for k, (b, y) in enumerate(GROUPS) if y == MINL]


def rows_at(unit, count=1):
    return pl.ds(pl.multiple_of(unit * BASE, BASE), count * BASE)


def plan_kernel(coarse, grids_each, lev_ref, out_ref):
    total_grids = lev_ref.shape[0]
    shared = []
    for b, y in GROUPS:
        holders = jnp.int32(0)
        for dev in range(total_grids // grids_each):
            held = jnp.int32(0)
            for c in range(dev * grids_each, (dev + 1) * grids_each):
                held = held | jnp.where((lev_ref[c, 0] >= b) & (lev_ref[c, 1] >= y), 1, 0)
            holders = holders + held
        shared.append(jnp.where(holders >= 2, 1, 0))
    count = jnp.int32(0)
    for k, units in enumerate(GROUP_UNITS):
        out_ref[k] = count
        count = count + shared[k] * units * coarse
    out_ref[len(GROUPS)] = count
    for k, units in enumerate(GROUP_UNITS):
        out_ref[k] = jnp.where(shared[k] == 1, out_ref[k], count)
        count = count + (1 - shared[k]) * units * coarse


def point_of(index, points):
    tier = jnp.where(index >= 4 * BASE, 4 * BASE, jnp.where(index >= 2 * BASE, 2 * BASE, BASE))
    step = jnp.where(index >= 4 * BASE, points >> 8, jnp.where(index >= 2 * BASE, points >> 7, points >> 6))
    fine = index >= BASE
    place = jnp.where(fine, (2 * (index - tier) + 1) * step, index * (points >> MINL))
    return place, jnp.where(fine, step, 0), fine


def front_kernel(dom_shift, lev_ref, vel_ref, rate_ref, v_ref, s_ref, u_ref, first_ref, last_ref):
    g = pl.program_id(0)
    lx = lev_ref[g, 0]
    points = jnp.int32(1) << lx
    live = jnp.int32(1) << (lx + lev_ref[g, 1] - dom_shift)
    nu = vel_ref[g, 0] * points.astype(jnp.float32) / LINE
    centre = 1.0 - nu * nu
    ahead = 0.5 * nu * nu - 0.5 * nu
    behind = 0.5 * nu * nu + 0.5 * nu
    damp = 1.0 - TAU * rate_ref[g]
    p = lax.broadcasted_iota(jnp.int32, (LINE, LINE), 0)
    q = lax.broadcasted_iota(jnp.int32, (LINE, LINE), 1)
    wrap = points - 1
    place, step, fine = point_of(p & wrap, points)
    same = (p >> lx) == (q >> lx)
    off = ((q & wrap) - place) & wrap
    lower = (off + step) & wrap
    upper = (off - step) & wrap
    half = jnp.where(fine, -0.5, 0.0)

    def adv(d):
        return jnp.where(d == 0, centre, jnp.where(d == 1, ahead, jnp.where(d == wrap, behind, 0.0)))

    def one(d):
        return jnp.where(d == 0, 1.0, 0.0)

    mat_v = jnp.where(same, damp * (adv(off) + half * (adv(lower) + adv(upper))), 0.0)
    mat_s = jnp.where(same, TAU * (one(off) + half * (one(lower) + one(upper))), 0.0)
    nt = (((1,), (1,)), ((), ()))
    last_block = jnp.maximum(live // LINE - 1, 0)
    for block in range(v_ref.shape[2] // LINE):
        @pl.when(block <= last_block)
        def _():
            cut = slice(block * LINE, (block + 1) * LINE)
            res = lax.dot_general(mat_v, v_ref[0, :, cut], nt, precision=EXACT, preferred_element_type=jnp.float32)
            res = res + lax.dot_general(mat_s, s_ref[0, :, cut], nt, precision=EXACT, preferred_element_type=jnp.float32)
            u_ref[0, cut, :] = res
            if block == 0:
                first_ref[0] = res

            @pl.when(block == last_block)
            def _():
                last_ref[0] = res


def y_coefs(nu):
    return 1.0 - nu * nu, 0.5 * nu * nu - 0.5 * nu, 0.5 * nu * nu + 0.5 * nu


def slot_of(start_ref, seg_shift, y, xu):
    inner = y & ((1 << seg_shift) - 1)
    step = inner & -inner
    step_shift = jnp.where(step >= 4, 2, jnp.where(step >= 2, 1, 0))
    ylev = jnp.where(inner == 0, 0, seg_shift - step_shift)
    index = jnp.where(inner == 0, y >> seg_shift, y >> (step_shift + 1))
    band = jnp.where(xu >= 4, 3, jnp.where(xu >= 2, 2, xu))
    group = jnp.where(band == 0, ylev, jnp.where(band == 1, 4 + ylev, jnp.where(band == 2, 7 + ylev, 9)))
    width_shift = jnp.where(band >= 2, band - 1, 0)
    first = jnp.where(band >= 2, 1 << width_shift, band)
    return start_ref[group] + (index << width_shift) + xu - first, step


def middle_kernel(dom_shift, lev_ref, vel_ref, coef_ref, start_ref, u_ref, next_ref, prev_ref, t_ref, ext, mov):
    g = pl.program_id(0)
    lx, ly = lev_ref[g, 0], lev_ref[g, 1]
    live = jnp.int32(1) << (lx + ly - dom_shift)
    units = live // BASE
    x_shift = lx - MINL
    nx = jnp.int32(1) << x_shift
    seg_shift = ly - MINL
    nu = vel_ref[g, 1] * (jnp.int32(1) << ly).astype(jnp.float32) / LINE
    centre, ahead, behind = y_coefs(nu)
    weight = coef_ref[g].astype(jnp.float32)
    halo_units = next_ref.shape[1] // BASE

    @pl.when(g == 0)
    def _():
        t_ref[...] = jnp.zeros_like(t_ref)

    prev_first = jnp.where(live < LINE, units, halo_units) - nx

    def take_prev(i, _):
        ext[rows_at(i), :] = prev_ref[0, rows_at(prev_first + i), :]
        return 0

    def take_own(i, _):
        ext[rows_at(nx + i), :] = u_ref[0, rows_at(i), :]
        return 0

    def take_next(i, _):
        ext[rows_at(nx + units + i), :] = next_ref[0, rows_at(i), :]
        return 0

    lax.fori_loop(0, nx, take_prev, 0)
    lax.fori_loop(0, units, take_own, 0)
    lax.fori_loop(0, jnp.minimum(2 * nx, jnp.minimum(units, halo_units)), take_next, 0)

    def step_y(i, _):
        mov[rows_at(i), :] = centre * ext[rows_at(i + nx), :] + ahead * ext[rows_at(i + 2 * nx), :] + behind * ext[rows_at(i), :]
        return 0

    lax.fori_loop(0, jnp.where(seg_shift > 0, units + nx, units), step_y, 0)

    def surplus(i, _):
        y, xu = i >> x_shift, i & (nx - 1)
        slot, step = slot_of(start_ref, seg_shift, y, xu)
        away = step << x_shift
        half = jnp.where(step > 0, 0.5, 0.0)
        value = mov[rows_at(i), :] - half * (mov[rows_at(i - away), :] + mov[rows_at(i + away), :])
        t_ref[rows_at(slot), :] = t_ref[rows_at(slot), :] + weight * value
        return 0

    lax.fori_loop(0, units, surplus, 0)


def pack_kernel(coarse, start_ref, t_ref, tail_ref, head_ref, sems):
    copies = []
    at = 0
    for k, (b, y) in enumerate(GROUPS):
        width = BAND_UNITS[b - MINL]
        last = start_ref[k] + (coarse * group_rows(y) - 1) * width
        copies.append((rows_at(last, width), tail_ref, slice(at * BASE, (at + width) * BASE)))
        at += width
    at = 0
    for k in HEAD_GROUPS:
        width = BAND_UNITS[GROUPS[k][0] - MINL]
        copies.append((rows_at(start_ref[k], width), head_ref, slice(at * BASE, (at + width) * BASE)))
        at += width
    moves = [pltpu.make_async_copy(t_ref.at[src, :], dst.at[cut, :], sems.at[n]) for n, (src, dst, cut) in enumerate(copies)]
    for move in moves:
        move.start()
    for move in moves:
        move.wait()


def back_kernel(dom_shift, lev_ref, vel_ref, start_ref, t_ref, tail_ref, head_ref, out_ref, val, comb):
    g = pl.program_id(0)
    lx, ly = lev_ref[g, 0], lev_ref[g, 1]
    live = jnp.int32(1) << (lx + ly - dom_shift)
    units = live // BASE
    x_shift = lx - MINL
    points = jnp.int32(1) << lx
    nx = jnp.int32(1) << x_shift
    seg_shift = ly - MINL
    nu = vel_ref[g, 1] * (jnp.int32(1) << ly).astype(jnp.float32) / LINE
    centre, ahead, behind = y_coefs(nu)

    def gather(i, _):
        slot, _step = slot_of(start_ref, seg_shift, i >> x_shift, i & (nx - 1))
        val[rows_at(nx + i), :] = t_ref[rows_at(slot), :]
        return 0

    lax.fori_loop(0, units, gather, 0)

    def edges(xu, _):
        after = val[rows_at(nx + xu), :]
        band = jnp.where(xu >= 4, 3, jnp.where(xu >= 2, 2, xu))
        width = jnp.where(band >= 2, 1 << (band - 1), 1)
        base = jnp.where(band == 0, 0, jnp.where(band == 1, 4 + xu - 1, jnp.where(band == 2, 7 + xu - 2, 11 + xu - 4)))

        def finer(tier, row):
            return tail_ref[rows_at(base + tier * width), :] + 0.5 * (row + after)

        val[rows_at(xu), :] = lax.fori_loop(1, seg_shift + 1, finer, tail_ref[rows_at(base), :])
        val[rows_at(nx + units + xu), :] = head_ref[rows_at(xu), :]
        return 0

    lax.fori_loop(0, nx, edges, 0)

    def tier_loop(tier, _):
        step_shift = seg_shift - tier
        away = jnp.int32(1) << (step_shift + x_shift)

        def lift(j, _):
            y = ((j >> x_shift) * 2 + 1) << step_shift
            i = nx + (y << x_shift) + (j & (nx - 1))
            val[rows_at(i), :] = val[rows_at(i), :] + 0.5 * (val[rows_at(i - away), :] + val[rows_at(i + away), :])
            return 0

        lax.fori_loop(0, units >> (step_shift + 1), lift, 0)
        return 0

    lax.fori_loop(1, seg_shift + 1, tier_loop, 0)

    def step_y(i, _):
        comb[rows_at(i), :] = centre * val[rows_at(i + nx), :] + ahead * val[rows_at(i + 2 * nx), :] + behind * val[rows_at(i), :]
        return 0

    lax.fori_loop(0, units, step_y, 0)

    def clear(i, _):
        comb[rows_at(i), :] = jnp.zeros((BASE, comb.shape[1]), jnp.float32)
        return 0

    lax.fori_loop(units, comb.shape[0] // BASE, clear, 0)

    p = lax.broadcasted_iota(jnp.int32, (LINE, LINE), 0)
    q = lax.broadcasted_iota(jnp.int32, (LINE, LINE), 1)
    wrap = points - 1
    place, step, fine = point_of(p & wrap, points)
    reach = jnp.where(fine, step, points >> MINL)
    inverse = jnp.where(fine, jnp.where(reach == 4, 0.25, jnp.where(reach == 2, 0.5, 1.0)), 1.0 / (points >> MINL).astype(jnp.float32))
    off = ((q & wrap) - place) & wrap
    apart = jnp.minimum(off, points - off)
    hat = jnp.maximum(0.0, 1.0 - apart.astype(jnp.float32) * inverse)
    mat = jnp.where((p >> lx) == (q >> lx), hat, 0.0)
    tn = (((0,), (0,)), ((), ()))
    for block in range(out_ref.shape[2] // LINE):
        cut = slice(block * LINE, (block + 1) * LINE)

        @pl.when(block * LINE < live)
        def _():
            out_ref[0, :, cut] = lax.dot_general(comb[cut, :], mat, tn, precision=EXACT, preferred_element_type=jnp.float32)

        @pl.when(block * LINE >= live)
        def _():
            out_ref[0, :, cut] = jnp.zeros((out_ref.shape[1], LINE), jnp.float32)


def sum_line(parts):
    count = lax.axis_size("grid")
    if count == 1:
        return parts
    if count % 2:
        return [lax.psum(part, "grid") for part in parts]
    half = count // 2
    z = lax.axis_index("grid")
    held = list(parts)
    for i in range(half - 1):
        held = [part + lax.ppermute(part, "grid", [(i, i + 1), (count - 1 - i, count - 2 - i)]) for part in held]
    held = [part + lax.ppermute(part, "grid", [(half - 1, half), (half, half - 1)]) for part in held]
    for i in range(half - 2, -1, -1):
        takes = (z == i) | (z == count - 1 - i)
        held = [jnp.where(takes, lax.ppermute(part, "grid", [(i + 1, i), (count - 2 - i, count - 1 - i)]), part) for part in held]
    return held


def sum_shared(sums, sizes, which, coarse):
    def branch(size, pieces):
        def run(t):
            bounds = [size * k // pieces * coarse * BASE for k in range(pieces + 1)]
            parts = sum_line([t[a:b] for a, b in zip(bounds, bounds[1:])])
            for a, part in zip(bounds, parts):
                t = lax.dynamic_update_slice(t, part, (a, 0))
            return t

        return run

    return lax.switch(which, [branch(size, 4) for size in sizes], sums)


SMEM = pl.BlockSpec(memory_space=pltpu.SMEM)


def whole(shape):
    return pl.BlockSpec(shape, lambda g: (0,) * len(shape))


def per_grid(shape):
    return pl.BlockSpec((1,) + shape, lambda g: (g, 0, 0))


def local(nodal_values, source_term, velocity, react_rate, levels, comb_coefs):
    grids, other, block_len = nodal_values.shape
    dom = lax.axis_size("dom")
    dom_shift = dom.bit_length() - 1
    coarse = BASE // dom
    params = pltpu.CompilerParams(vmem_limit_bytes=VMEM_BYTES)
    f32 = jnp.float32
    all_levels = lax.all_gather(levels, "grid", tiled=True)

    values, first, last = pl.pallas_call(
        functools.partial(front_kernel, dom_shift),
        grid=(grids,),
        in_specs=[SMEM, SMEM, SMEM, per_grid((other, block_len)), per_grid((other, block_len))],
        out_specs=[per_grid((block_len, other)), per_grid((LINE, other)), per_grid((LINE, other))],
        out_shape=[
            jax.ShapeDtypeStruct((grids, block_len, other), f32),
            jax.ShapeDtypeStruct((grids, LINE, other), f32),
            jax.ShapeDtypeStruct((grids, LINE, other), f32),
        ],
        compiler_params=params,
        name="front",
    )(levels, velocity, react_rate, nodal_values, source_term)

    to_next = [(i, (i + 1) % dom) for i in range(dom)]
    to_prev = [(i, (i - 1) % dom) for i in range(dom)]
    after = lax.ppermute(first, "dom", to_prev)
    before = lax.ppermute(last, "dom", to_next)

    starts = pl.pallas_call(
        functools.partial(plan_kernel, coarse, grids),
        in_specs=[SMEM],
        out_specs=SMEM,
        out_shape=jax.ShapeDtypeStruct((len(GROUPS) + 1,), jnp.int32),
        name="plan",
    )(all_levels)

    sum_rows = TOTAL_UNITS * coarse * BASE
    sums = pl.pallas_call(
        functools.partial(middle_kernel, dom_shift),
        grid=(grids,),
        in_specs=[SMEM, SMEM, SMEM, SMEM, per_grid((block_len, other)), per_grid((LINE, other)), per_grid((LINE, other))],
        out_specs=whole((sum_rows, other)),
        out_shape=jax.ShapeDtypeStruct((sum_rows, other), f32),
        scratch_shapes=[pltpu.VMEM((block_len + 3 * LINE, other), f32), pltpu.VMEM((block_len + LINE, other), f32)],
        compiler_params=params,
        name="middle",
    )(levels, velocity, comb_coefs, starts, values, after, before)

    sizes = [5, 6, 7, 8, 9, 10, 11, 12, 13, 14, 16, TOTAL_UNITS]
    limits = jnp.asarray([size * coarse for size in sizes[:-1]], jnp.int32)
    which = jnp.sum((starts[len(GROUPS)] > limits).astype(jnp.int32))
    sums = sum_shared(sums, sizes, which, coarse)

    any_space = pl.BlockSpec(memory_space=pl.ANY)
    tail_rows = sum(BAND_UNITS[b - MINL] for b, _ in GROUPS) * BASE
    head_rows = sum(BAND_UNITS) * BASE
    tail, head = pl.pallas_call(
        functools.partial(pack_kernel, coarse),
        in_specs=[SMEM, any_space],
        out_specs=[any_space, any_space],
        out_shape=[jax.ShapeDtypeStruct((tail_rows, other), f32), jax.ShapeDtypeStruct((head_rows, other), f32)],
        scratch_shapes=[pltpu.SemaphoreType.DMA((len(GROUPS) + len(HEAD_GROUPS),))],
        compiler_params=params,
        name="pack",
    )(starts, sums)
    tail = lax.ppermute(tail, "dom", to_next)
    head = lax.ppermute(head, "dom", to_prev)

    return pl.pallas_call(
        functools.partial(back_kernel, dom_shift),
        grid=(grids,),
        in_specs=[SMEM, SMEM, SMEM, whole((sum_rows, other)), whole((tail_rows, other)), whole((head_rows, other))],
        out_specs=per_grid((other, block_len)),
        out_shape=jax.ShapeDtypeStruct((grids, other, block_len), f32),
        scratch_shapes=[pltpu.VMEM((block_len + 2 * LINE, other), f32), pltpu.VMEM((block_len, other), f32)],
        compiler_params=params,
        name="back",
    )(levels, velocity, starts, sums, tail, head)


def solution(mesh):
    in_specs = (
        P("grid", None, "dom"),
        P("grid", None, "dom"),
        P("grid", None),
        P("grid"),
        P("grid", None),
        P("grid"),
    )
    return jax.shard_map(local, mesh=mesh, in_specs=in_specs, out_specs=P("grid", None, "dom"), check_vma=False)
```

```python
import functools
import itertools

import jax
import jax.numpy as jnp
from jax import lax
from jax.experimental import pallas as pl
from jax.experimental.pallas import tpu as pltpu
from jax.sharding import PartitionSpec as P

MAXL = 8
MINL = 5
LSUM = 13
LINE = 2**MAXL
BASE = 2**MINL
TAU = 0.25
VMEM_BYTES = 48 * 2**20
CHUNK = 2
BRANCHES = [2, 3, 4, 5, 6, 7, 8]

GROUPS = [(b, y) for b in range(MINL, MAXL + 1) for y in range(MINL, LSUM - b + 1)]
BAND_UNITS = [1] + [2**t for t in range(MAXL - MINL)]
BAND_FIRST = [0] + [2**t for t in range(MAXL - MINL)]


def group_rows(y):
    return 1 if y == MINL else 2 ** (y - MINL - 1)


GROUP_UNITS = [group_rows(y) * BAND_UNITS[b - MINL] for b, y in GROUPS]
TOTAL_UNITS = sum(GROUP_UNITS)
HEAD_GROUPS = [k for k, (b, y) in enumerate(GROUPS) if y == MINL]


def rows_at(unit, count=1):
    return pl.ds(pl.multiple_of(unit * BASE, BASE), count * BASE)


def region_units(y, coarse):
    rows = group_rows(y) * coarse
    return max(rows - 2, 0), min(rows, 2)


def group_sizes(coarse):
    inner, edge = zip(*[region_units(y, coarse) for _, y in GROUPS])
    widths = [BAND_UNITS[b - MINL] for b, _ in GROUPS]
    return [n * w for n, w in zip(inner, widths)], [n * w for n, w in zip(edge, widths)]


def branch_table(coarse, chunk):
    inner, edge = group_sizes(coarse)
    tops = [[-1] + list(range(MINL, LSUM - b + 1)) for b in range(MINL, MAXL + 1)]
    cases = []
    for top in itertools.product(*tops):
        if all(hi >= lo for hi, lo in zip(top, top[1:])):
            held = [y <= top[b - MINL] for b, y in GROUPS]
            cases.append((sum(n for n, h in zip(inner, held) if h), sum(n for n, h in zip(edge, held) if h)))
    total = -(-TOTAL_UNITS * coarse // chunk)
    table, low = [], -1
    for count in [c for c in BRANCHES if c < total] + [total]:
        fits = [i for i, e in cases if low < i + e <= count * chunk]
        table.append((count, min(fits) // chunk if fits else 0))
        low = count * chunk
    return table


def plan_kernel(coarse, limits, *refs):
    *lev_refs, start_ref, which_ref = refs
    shared = []
    for b, y in GROUPS:
        holders = jnp.int32(0)
        for lev_ref in lev_refs:
            held = jnp.int32(0)
            for c in range(lev_ref.shape[0]):
                held = held | jnp.where((lev_ref[c, 0] >= b) & (lev_ref[c, 1] >= y), 1, 0)
            holders = holders + held
        shared.append(jnp.where(holders >= 2, 1, 0))
    inner, edge = group_sizes(coarse)
    starts = [jnp.int32(0)] * (2 * len(GROUPS))
    count = jnp.int32(0)
    for wanted in (1, 0):
        for n, size in enumerate(inner + edge):
            take = shared[n % len(GROUPS)] == wanted
            starts[n] = jnp.where(take, count, starts[n])
            count = count + jnp.where(take, size, 0)
        if wanted:
            which = jnp.int32(0)
            for limit in limits:
                which = which + jnp.where(count > limit, 1, 0)
            which_ref[0] = which
    for n, start in enumerate(starts):
        start_ref[n] = start


def point_of(index, points):
    tier = jnp.where(index >= 4 * BASE, 4 * BASE, jnp.where(index >= 2 * BASE, 2 * BASE, BASE))
    step = jnp.where(index >= 4 * BASE, points >> 8, jnp.where(index >= 2 * BASE, points >> 7, points >> 6))
    fine = index >= BASE
    place = jnp.where(fine, (2 * (index - tier) + 1) * step, index * (points >> MINL))
    return place, jnp.where(fine, step, 0), fine


def halves(x):
    high = x.astype(jnp.bfloat16)
    return high, (x - high.astype(jnp.float32)).astype(jnp.bfloat16)


def dot(a, b, dims):
    return lax.dot_general(a, b, dims, preferred_element_type=jnp.float32)


def front_kernel(dom_shift, lev_ref, vel_ref, rate_ref, v_ref, s_ref, u_ref, first_ref, last_ref):
    g = pl.program_id(0)
    lx = lev_ref[g, 0]
    points = jnp.int32(1) << lx
    live = jnp.int32(1) << (lx + lev_ref[g, 1] - dom_shift)
    nu = vel_ref[g, 0] * points.astype(jnp.float32) / LINE
    centre = 1.0 - nu * nu
    ahead = 0.5 * nu * nu - 0.5 * nu
    behind = 0.5 * nu * nu + 0.5 * nu
    damp = 1.0 - TAU * rate_ref[g]
    p = lax.broadcasted_iota(jnp.int32, (LINE, LINE), 0)
    q = lax.broadcasted_iota(jnp.int32, (LINE, LINE), 1)
    wrap = points - 1
    place, step, fine = point_of(p & wrap, points)
    same = (p >> lx) == (q >> lx)
    off = ((q & wrap) - place) & wrap
    lower = (off + step) & wrap
    upper = (off - step) & wrap
    half = jnp.where(fine, -0.5, 0.0)

    def adv(d):
        return jnp.where(d == 0, centre, jnp.where(d == 1, ahead, jnp.where(d == wrap, behind, 0.0)))

    def one(d):
        return jnp.where(d == 0, 1.0, 0.0)

    mat_v = jnp.where(same, damp * (adv(off) + half * (adv(lower) + adv(upper))), 0.0)
    mat_hi, mat_lo = halves(mat_v)
    mat_s = jnp.where(same, TAU * (one(off) + half * (one(lower) + one(upper))), 0.0).astype(jnp.bfloat16)
    nt = (((1,), (1,)), ((), ()))
    last_block = jnp.maximum(live // LINE - 1, 0)
    for block in range(v_ref.shape[2] // LINE):
        @pl.when(block <= last_block)
        def _():
            cut = slice(block * LINE, (block + 1) * LINE)
            v_hi, v_lo = halves(v_ref[0, :, cut])
            s_hi, s_lo = halves(s_ref[0, :, cut])
            res = dot(mat_hi, v_hi, nt) + dot(mat_lo, v_hi, nt) + dot(mat_hi, v_lo, nt) + dot(mat_s, s_hi, nt) + dot(mat_s, s_lo, nt)
            u_ref[0, cut, :] = res
            if block == 0:
                first_ref[0] = res

            @pl.when(block == last_block)
            def _():
                last_ref[0] = res


def y_coefs(nu):
    return 1.0 - nu * nu, 0.5 * nu * nu - 0.5 * nu, 0.5 * nu * nu + 0.5 * nu


def group_of(tier, xu):
    band = jnp.where(xu >= 4, 3, jnp.where(xu >= 2, 2, xu))
    group = jnp.where(band == 0, tier, jnp.where(band == 1, 4 + tier, jnp.where(band == 2, 7 + tier, 9)))
    width = jnp.where(band >= 2, 1 << (band - 1), 1)
    return group, width, xu - jnp.where(band >= 2, width, band)


class Shape:
    def __init__(self, lev_ref, g, dom_shift):
        self.lx, self.ly = lev_ref[g, 0], lev_ref[g, 1]
        self.live = jnp.int32(1) << (self.lx + self.ly - dom_shift)
        self.units = self.live // BASE
        self.x_shift = self.lx - MINL
        self.nx = jnp.int32(1) << self.x_shift
        self.points = jnp.int32(1) << self.lx
        self.seg_shift = self.ly - MINL
        self.rows = self.units >> self.x_shift

    def tier(self, tier):
        step = jnp.int32(1) << (self.seg_shift - tier)
        fine = tier > 0
        count = jnp.where(fine, self.rows >> (self.seg_shift - tier + 1), self.rows >> self.seg_shift)
        return count, jnp.where(fine, step, 0), jnp.where(fine, step, 0), jnp.where(fine, 2 * step, step)


def add_surplus(t_ref, mov, shape, tier, y, xu, step, slot, weight):
    i = (y << shape.x_shift) + xu
    away = step << shape.x_shift
    half = jnp.where(step > 0, 0.5, 0.0)
    value = mov[rows_at(i), :] - half * (mov[rows_at(i - away), :] + mov[rows_at(i + away), :])
    t_ref[rows_at(slot), :] = t_ref[rows_at(slot), :] + weight * value


def send_out(t_ref, out_refs, sems):
    moves, at = [], 0
    for n, out_ref in enumerate(out_refs):
        size = out_ref.shape[0]
        moves.append(pltpu.make_async_copy(t_ref.at[at : at + size, :], out_ref, sems.at[n]))
        at += size
    for move in moves:
        move.start()
    for move in moves:
        move.wait()


def inner_kernel(dom_shift, n_out, lev_ref, vel_ref, coef_ref, start_ref, u_ref, *refs):
    out_refs, (t_ref, mov, sems) = refs[:n_out], refs[n_out:]
    t_ref[...] = jnp.zeros_like(t_ref)
    for g in range(u_ref.shape[0]):
        shape = Shape(lev_ref, g, dom_shift)
        nx, x_shift = shape.nx, shape.x_shift
        centre, ahead, behind = y_coefs(vel_ref[g, 1] * (jnp.int32(1) << shape.ly).astype(jnp.float32) / LINE)
        weight = coef_ref[g].astype(jnp.float32)

        def step_y(n, _):
            i = nx + 2 * n
            mov[rows_at(i, 2), :] = (
                centre * u_ref[g, rows_at(i, 2), :] + ahead * u_ref[g, rows_at(i + nx, 2), :] + behind * u_ref[g, rows_at(i - nx, 2), :]
            )
            return 0

        lax.fori_loop(0, jnp.maximum(shape.units - 2 * nx, 0) >> 1, step_y, 0)

        def tier_loop(tier, _):
            count, step, first, stride = shape.tier(tier)

            def one(n, _):
                j, xu = (n >> x_shift) + 1, n & (nx - 1)
                group, width, place = group_of(tier, xu)
                slot = start_ref[group] + (j - 1) * width + place
                add_surplus(t_ref, mov, shape, tier, first + j * stride, xu, step, slot, weight)
                return 0

            lax.fori_loop(0, jnp.maximum(count - 2, 0) << x_shift, one, 0)
            return 0

        lax.fori_loop(0, shape.seg_shift + 1, tier_loop, 0)
    send_out(t_ref, out_refs, sems)


def edge_kernel(dom_shift, n_out, sent, lev_ref, vel_ref, coef_ref, start_ref, u_ref, rest_ref, next_ref, prev_ref, *refs):
    out_refs, (t_ref, mov, sems) = refs[:n_out], refs[n_out:]
    load = pltpu.make_async_copy(rest_ref, t_ref, sems.at[n_out])
    load.start()
    halo_units = next_ref.shape[1] // BASE
    for g in range(u_ref.shape[0]):
        shape = Shape(lev_ref, g, dom_shift)
        nx, x_shift, units, rows = shape.nx, shape.x_shift, shape.units, shape.rows
        centre, ahead, behind = y_coefs(vel_ref[g, 1] * (jnp.int32(1) << shape.ly).astype(jnp.float32) / LINE)
        weight = coef_ref[g].astype(jnp.float32)
        prev_first = jnp.where(shape.live < LINE, units, halo_units) - nx

        def ends(xu, _):
            before = prev_ref[g, rows_at(prev_first + xu), :]
            head = u_ref[g, rows_at(xu), :]
            last = u_ref[g, rows_at(units - nx + xu), :]
            after = next_ref[g, rows_at(xu), :]

            @pl.when(rows == 1)
            def _():
                mov[rows_at(xu), :] = centre * head + ahead * after + behind * before

            @pl.when(rows > 1)
            def _():
                mov[rows_at(xu), :] = centre * head + ahead * u_ref[g, rows_at(nx + xu), :] + behind * before
                mov[rows_at(units - nx + xu), :] = centre * last + ahead * after + behind * u_ref[g, rows_at(units - 2 * nx + xu), :]

            @pl.when(shape.seg_shift > 0)
            def _():
                mov[rows_at(units + xu), :] = centre * after + ahead * next_ref[g, rows_at(nx + xu), :] + behind * last

            return 0

        lax.fori_loop(0, nx, ends, 0)

        def step_y(i, _):
            mov[rows_at(i), :] = centre * u_ref[g, rows_at(i), :] + ahead * u_ref[g, rows_at(i + nx), :] + behind * u_ref[g, rows_at(i - nx), :]
            return 0

        segment = jnp.int32(1) << shape.seg_shift
        near = jnp.minimum(segment, rows - 2)
        lax.fori_loop(nx, (near + 1) << x_shift, step_y, 0)
        lax.fori_loop(jnp.maximum(rows - segment, near + 1) << x_shift, (rows - 1) << x_shift, step_y, 0)
        if g == 0:
            load.wait()

        def tier_loop(tier, _):
            count, step, first, stride = shape.tier(tier)

            def one(n, _):
                end, xu = n >> x_shift, n & (nx - 1)
                group, width, place = group_of(tier, xu)
                slot = start_ref[len(GROUPS) + group] + end * width + place - sent
                add_surplus(t_ref, mov, shape, tier, first + end * (count - 1) * stride, xu, step, slot, weight)
                return 0

            lax.fori_loop(0, jnp.minimum(count, 2) << x_shift, one, 0)
            return 0

        lax.fori_loop(0, shape.seg_shift + 1, tier_loop, 0)
    send_out(t_ref, out_refs, sems)


def load_sums(t_ref, got, rest_ref, sems, first=0):
    count = lax.axis_size("grid")
    z = lax.axis_index("grid")
    passed_on = (z == 0) | (z == count - 1)
    at = 0
    waits = []
    for n, (total, passed) in enumerate(got):
        size = total.shape[0]
        dst = t_ref.at[at : at + size, :]
        if passed is None:
            pltpu.make_async_copy(total, dst, sems.at[n]).start()
        else:
            @pl.when(passed_on)
            def _():
                pltpu.make_async_copy(passed, dst, sems.at[n]).start()

            @pl.when(jnp.logical_not(passed_on))
            def _():
                pltpu.make_async_copy(total, dst, sems.at[n]).start()
        waits.append(pltpu.make_async_copy(total, dst, sems.at[n]))
        at += size
    if rest_ref is not None:
        waits.append(pltpu.make_async_copy(rest_ref, t_ref.at[at : at + rest_ref.shape[0], :], sems.at[len(got)]))
        waits[-1].start()
    for wait in waits:
        wait.wait()


def pairs_of(refs, count, paired):
    if paired:
        return [(refs[2 * n], refs[2 * n + 1]) for n in range(count)], refs[2 * count :]
    return [(refs[n], None) for n in range(count)], refs[count:]


def pack_kernel(coarse, sent, count, paired, has_rest, start_ref, *refs):
    got, refs = pairs_of(refs, count, paired)
    rest_ref, refs = (refs[0], refs[1:]) if has_rest else (None, refs)
    tail_ref, head_ref, t_ref, sems = refs
    load_sums(t_ref, got, rest_ref, sems)
    at = 0
    for k, (b, y) in enumerate(GROUPS):
        width = BAND_UNITS[b - MINL]
        last = start_ref[len(GROUPS) + k] + (region_units(y, coarse)[1] - 1) * width - sent
        tail_ref[at * BASE : (at + width) * BASE, :] = t_ref[rows_at(last, width), :]
        at += width
    at = 0
    for k in HEAD_GROUPS:
        width = BAND_UNITS[GROUPS[k][0] - MINL]
        head_ref[at * BASE : (at + width) * BASE, :] = t_ref[rows_at(start_ref[len(GROUPS) + k] - sent, width), :]
        at += width


def back_kernel(dom_shift, count, paired, has_rest, lev_ref, vel_ref, start_ref, tail_ref, head_ref, *refs):
    got, refs = pairs_of(refs, count, paired)
    rest_ref, refs = (refs[0], refs[1:]) if has_rest else (None, refs)
    out_ref, t_ref, val, comb, sems = refs
    g = pl.program_id(0)

    @pl.when(g == 0)
    def _():
        load_sums(t_ref, got, rest_ref, sems)

    shape = Shape(lev_ref, g, dom_shift)
    nx, x_shift, units, points, live, seg_shift, lx = shape.nx, shape.x_shift, shape.units, shape.points, shape.live, shape.seg_shift, shape.lx
    centre, ahead, behind = y_coefs(vel_ref[g, 1] * (jnp.int32(1) << shape.ly).astype(jnp.float32) / LINE)

    def gather_tier(tier, _):
        rows, step, first, stride = shape.tier(tier)

        def one(n, _):
            j, xu = n >> x_shift, n & (nx - 1)
            group, width, place = group_of(tier, xu)
            inner = (j > 0) & (j < rows - 1)
            slot = jnp.where(inner, start_ref[group] + (j - 1) * width, start_ref[len(GROUPS) + group] + jnp.where(j > 0, width, 0)) + place
            val[rows_at(nx + ((first + j * stride) << x_shift) + xu), :] = t_ref[rows_at(slot), :]
            return 0

        lax.fori_loop(0, rows << x_shift, one, 0)
        return 0

    lax.fori_loop(0, seg_shift + 1, gather_tier, 0)

    def edges(xu, _):
        after = val[rows_at(nx + xu), :]
        band = jnp.where(xu >= 4, 3, jnp.where(xu >= 2, 2, xu))
        width = jnp.where(band >= 2, 1 << (band - 1), 1)
        base = jnp.where(band == 0, 0, jnp.where(band == 1, 4 + xu - 1, jnp.where(band == 2, 7 + xu - 2, 11 + xu - 4)))

        def finer(tier, row):
            return tail_ref[rows_at(base + tier * width), :] + 0.5 * (row + after)

        val[rows_at(xu), :] = lax.fori_loop(1, seg_shift + 1, finer, tail_ref[rows_at(base), :])
        val[rows_at(nx + units + xu), :] = head_ref[rows_at(xu), :]
        return 0

    lax.fori_loop(0, nx, edges, 0)

    def tier_loop(tier, _):
        step_shift = seg_shift - tier
        away = jnp.int32(1) << (step_shift + x_shift)

        def lift(j, _):
            y = ((j >> x_shift) * 2 + 1) << step_shift
            i = nx + (y << x_shift) + (j & (nx - 1))
            val[rows_at(i), :] = val[rows_at(i), :] + 0.5 * (val[rows_at(i - away), :] + val[rows_at(i + away), :])
            return 0

        lax.fori_loop(0, units >> (step_shift + 1), lift, 0)
        return 0

    lax.fori_loop(1, seg_shift + 1, tier_loop, 0)

    def step_y(i, _):
        comb[rows_at(i), :] = centre * val[rows_at(i + nx), :] + ahead * val[rows_at(i + 2 * nx), :] + behind * val[rows_at(i), :]
        return 0

    lax.fori_loop(0, units, step_y, 0)

    def clear(i, _):
        comb[rows_at(i), :] = jnp.zeros((BASE, comb.shape[1]), jnp.float32)
        return 0

    lax.fori_loop(units, comb.shape[0] // BASE, clear, 0)

    p = lax.broadcasted_iota(jnp.int32, (LINE, LINE), 0)
    q = lax.broadcasted_iota(jnp.int32, (LINE, LINE), 1)
    wrap = points - 1
    place, step, fine = point_of(p & wrap, points)
    reach = jnp.where(fine, step, points >> MINL)
    inverse = jnp.where(fine, jnp.where(reach == 4, 0.25, jnp.where(reach == 2, 0.5, 1.0)), 1.0 / (points >> MINL).astype(jnp.float32))
    off = ((q & wrap) - place) & wrap
    apart = jnp.minimum(off, points - off)
    hat = jnp.maximum(0.0, 1.0 - apart.astype(jnp.float32) * inverse)
    mat = jnp.where((p >> lx) == (q >> lx), hat, 0.0)
    mat = mat.astype(jnp.bfloat16)
    tn = (((0,), (0,)), ((), ()))
    for block in range(out_ref.shape[2] // LINE):
        cut = slice(block * LINE, (block + 1) * LINE)

        @pl.when(block * LINE < live)
        def _():
            high, low = halves(comb[cut, :])
            out_ref[0, :, cut] = dot(high, mat, tn) + dot(low, mat, tn)

        @pl.when(block * LINE >= live)
        def _():
            out_ref[0, :, cut] = jnp.zeros((out_ref.shape[1], LINE), jnp.float32)


def sum_line(parts):
    count = lax.axis_size("grid")
    if count == 1:
        return [(part, None) for part in parts]
    if count % 2:
        return [(lax.psum(part, "grid"), None) for part in parts]
    half = count // 2
    z = lax.axis_index("grid")
    arrived = [lax.ppermute(part, "grid", [(0, 1), (count - 1, count - 2)]) if half > 1 else None for part in parts]
    done = [None] * len(parts)
    held = [None] * len(parts)

    def inward(n):
        total = parts[n] if arrived[n] is None else parts[n] + arrived[n]
        for i in range(1, half - 1):
            total = total + lax.ppermute(total, "grid", [(i, i + 1), (count - 1 - i, count - 2 - i)])
        held[n] = total

    def outward(n, crossed):
        total = held[n] + crossed
        for i in range(half - 2, 0, -1):
            came = lax.ppermute(total, "grid", [(i + 1, i), (count - 2 - i, count - 1 - i)])
            total = jnp.where((z == i) | (z == count - 1 - i), came, total)
        passed = lax.ppermute(total, "grid", [(1, 0), (count - 2, count - 1)]) if half > 1 else None
        done[n] = (total, passed)

    crossed = [None] * len(parts)
    for n in range(len(parts) + 1):
        if n < len(parts):
            if n >= 1 and arrived[n] is not None:
                arrived[n], held[n - 1] = lax.optimization_barrier((arrived[n], held[n - 1]))
            inward(n)
            crossed[n] = lax.ppermute(held[n], "grid", [(half - 1, half), (half, half - 1)])
        if n >= 1:
            if n < len(parts):
                crossed[n - 1], held[n] = lax.optimization_barrier((crossed[n - 1], held[n]))
            outward(n - 1, crossed[n - 1])
            if n + 1 < len(parts) and arrived[n + 1] is not None:
                arrived[n + 1], keep = lax.optimization_barrier((arrived[n + 1], done[n - 1][0]))
                done[n - 1] = (keep, done[n - 1][1])
    return done


SMEM = pl.BlockSpec(memory_space=pltpu.SMEM)
VMEM = pl.BlockSpec(memory_space=pltpu.VMEM)
ANY = pl.BlockSpec(memory_space=pl.ANY)


def per_grid(shape):
    return pl.BlockSpec((1,) + shape, lambda g: (g, 0, 0))


def run_branch(dom, sent, inner, operands):
    levels, velocity, comb_coefs, starts, values, first, last = operands
    f32 = jnp.float32
    grids, block_len, other = values.shape
    dom_shift = dom.bit_length() - 1
    coarse = BASE // dom
    chunk = CHUNK * coarse * BASE
    rest = TOTAL_UNITS * coarse * BASE - sent * chunk
    later = sent - inner
    params = pltpu.CompilerParams(vmem_limit_bytes=VMEM_BYTES)
    to_next = [(i, (i + 1) % dom) for i in range(dom)]
    to_prev = [(i, (i - 1) % dom) for i in range(dom)]

    def rows(n):
        return jax.ShapeDtypeStruct((n, other), f32)

    after = lax.ppermute(first, "dom", to_prev)
    before = lax.ppermute(last, "dom", to_next)

    outs = [rows(chunk)] * inner + [rows(later * chunk + rest)]
    *parts, held = pl.pallas_call(
        functools.partial(inner_kernel, dom_shift, len(outs)),
        in_specs=[SMEM] * 4 + [VMEM],
        out_specs=[ANY] * len(outs),
        out_shape=outs,
        scratch_shapes=[
            pltpu.VMEM((TOTAL_UNITS * coarse * BASE, other), f32),
            pltpu.VMEM((block_len + LINE, other), f32),
            pltpu.SemaphoreType.DMA((len(outs),)),
        ],
        compiler_params=params,
        name="inner",
    )(levels, velocity, comb_coefs, starts, values)

    outs = [rows(chunk)] * later + [rows(rest)] * (rest > 0)
    edges = list(pl.pallas_call(
        functools.partial(edge_kernel, dom_shift, len(outs), inner * chunk // BASE),
        in_specs=[SMEM] * 4 + [VMEM, ANY, VMEM, VMEM],
        out_specs=[ANY] * len(outs),
        out_shape=outs,
        scratch_shapes=[
            pltpu.VMEM((later * chunk + rest, other), f32),
            pltpu.VMEM((block_len + LINE, other), f32),
            pltpu.SemaphoreType.DMA((len(outs) + 1,)),
        ],
        compiler_params=params,
        name="edge",
    )(levels, velocity, comb_coefs, starts, values, held, after, before))
    own = edges[later:]
    parts = parts + edges[:later]

    order = list(range(sent)) if inner < 2 else list(range(inner - 1)) + list(range(inner, sent)) + [inner - 1]
    summed = dict(zip(order, sum_line([parts[n] for n in order])))
    paired = summed[0][1] is not None
    flat = [x for n in range(sent) for x in summed[n] if x is not None]
    flat_later = [x for n in range(inner, sent) for x in summed[n] if x is not None]

    tail_rows = sum(BAND_UNITS[b - MINL] for b, _ in GROUPS) * BASE
    head_rows = sum(BAND_UNITS) * BASE
    tail, head = pl.pallas_call(
        functools.partial(pack_kernel, coarse, inner * chunk // BASE, later, paired, rest > 0),
        in_specs=[SMEM] + [ANY] * (len(flat_later) + len(own)),
        out_specs=[VMEM, VMEM],
        out_shape=[rows(tail_rows), rows(head_rows)],
        scratch_shapes=[pltpu.VMEM((later * chunk + rest, other), f32), pltpu.SemaphoreType.DMA((later + 1,))],
        compiler_params=params,
        name="pack",
    )(starts, *flat_later, *own)
    tail = lax.ppermute(tail, "dom", to_next)
    head = lax.ppermute(head, "dom", to_prev)

    return pl.pallas_call(
        functools.partial(back_kernel, dom_shift, sent, paired, rest > 0),
        grid=(grids,),
        in_specs=[SMEM] * 3 + [VMEM, VMEM] + [ANY] * (len(flat) + len(own)),
        out_specs=per_grid((other, block_len)),
        out_shape=jax.ShapeDtypeStruct((grids, other, block_len), f32),
        scratch_shapes=[
            pltpu.VMEM((sent * chunk + rest, other), f32),
            pltpu.VMEM((block_len + 2 * LINE, other), f32),
            pltpu.VMEM((block_len, other), f32),
            pltpu.SemaphoreType.DMA((sent + 1,)),
        ],
        compiler_params=params,
        name="back",
    )(levels, velocity, starts, tail, head, *flat, *own)


def local(nodal_values, source_term, velocity, react_rate, levels, comb_coefs):
    grids, other, block_len = nodal_values.shape
    dom = lax.axis_size("dom")
    count = lax.axis_size("grid")
    dom_shift = dom.bit_length() - 1
    coarse = BASE // dom
    f32 = jnp.float32
    all_levels = [levels] + [lax.ppermute(levels, "grid", [(i, (i + k) % count) for i in range(count)]) for k in range(1, count)]

    values, first, last = pl.pallas_call(
        functools.partial(front_kernel, dom_shift),
        grid=(grids,),
        in_specs=[SMEM, SMEM, SMEM, per_grid((other, block_len)), per_grid((other, block_len))],
        out_specs=[per_grid((block_len, other)), per_grid((LINE, other)), per_grid((LINE, other))],
        out_shape=[
            jax.ShapeDtypeStruct((grids, block_len, other), f32),
            jax.ShapeDtypeStruct((grids, LINE, other), f32),
            jax.ShapeDtypeStruct((grids, LINE, other), f32),
        ],
        compiler_params=pltpu.CompilerParams(vmem_limit_bytes=VMEM_BYTES),
        name="front",
    )(levels, velocity, react_rate, nodal_values, source_term)

    table = branch_table(coarse, CHUNK * coarse)
    starts, which = pl.pallas_call(
        functools.partial(plan_kernel, coarse, [sent * CHUNK * coarse for sent, _ in table[:-1]]),
        in_specs=[SMEM] * count,
        out_specs=[SMEM, SMEM],
        out_shape=[jax.ShapeDtypeStruct((2 * len(GROUPS),), jnp.int32), jax.ShapeDtypeStruct((1,), jnp.int32)],
        name="plan",
    )(*all_levels)

    operands = (levels, velocity, comb_coefs, starts, values, first, last)
    branches = [functools.partial(run_branch, dom, sent, inner) for sent, inner in table]
    return lax.switch(which[0], branches, operands)


def solution(mesh):
    in_specs = (
        P("grid", None, "dom"),
        P("grid", None, "dom"),
        P("grid", None),
        P("grid"),
        P("grid", None),
        P("grid"),
    )
    return jax.shard_map(local, mesh=mesh, in_specs=in_specs, out_specs=P("grid", None, "dom"), check_vma=False)
```

```python
import functools
import itertools

import jax
import jax.numpy as jnp
from jax import lax
from jax.experimental import pallas as pl
from jax.experimental.pallas import tpu as pltpu
from jax.sharding import PartitionSpec as P

MAXL = 8
MINL = 5
LSUM = 13
LINE = 2**MAXL
BASE = 2**MINL
TAU = 0.25
VMEM_BYTES = 48 * 2**20
VMEM_MOST = 63 * 2**20
BRANCHES = [(4, 2), (6, 3), (7, 4), (8, 4), (10, 5), (12, 4), (14, 5)]
AHEAD = 3
EARLY = 1

GROUPS = [(b, y) for b in range(MINL, MAXL + 1) for y in range(MINL, LSUM - b + 1)]
BAND_UNITS = [1] + [2**t for t in range(MAXL - MINL)]
BAND_FIRST = [0] + [2**t for t in range(MAXL - MINL)]


def group_rows(y):
    return 1 if y == MINL else 2 ** (y - MINL - 1)


GROUP_UNITS = [group_rows(y) * BAND_UNITS[b - MINL] for b, y in GROUPS]
TOTAL_UNITS = sum(GROUP_UNITS)
HEAD_GROUPS = [k for k, (b, y) in enumerate(GROUPS) if y == MINL]


def rows_at(unit, count=1):
    return pl.ds(pl.multiple_of(unit * BASE, BASE), count * BASE)


def region_units(y, coarse):
    rows = group_rows(y) * coarse
    return max(rows - 2, 0), min(rows, 2)


def group_sizes(coarse):
    inner, edge = zip(*[region_units(y, coarse) for _, y in GROUPS])
    widths = [BAND_UNITS[b - MINL] for b, _ in GROUPS]
    return [n * w for n, w in zip(inner, widths)], [n * w for n, w in zip(edge, widths)]


def branch_table(coarse):
    inner, edge = group_sizes(coarse)
    tops = [[-1] + list(range(MINL, LSUM - b + 1)) for b in range(MINL, MAXL + 1)]
    cases = []
    for top in itertools.product(*tops):
        if all(hi >= lo for hi, lo in zip(top, top[1:])):
            held = [y <= top[b - MINL] for b, y in GROUPS]
            cases.append((sum(n for n, h in zip(inner, held) if h), sum(n for n, h in zip(edge, held) if h)))
    table, low = [], -1
    for size, count in BRANCHES + [(TOTAL_UNITS, TOTAL_UNITS // 2)]:
        chunk = -(-size * coarse // count)
        top = count * chunk
        fits = [(i, e) for i, e in cases if low < i + e <= top]
        if fits:
            before = min(min(i for i, _ in fits) // chunk, EARLY)
            spill = any(top > sum(inner) + e and e < sum(edge) for _, e in fits)
            end = count if spill else before - (-max(e for _, e in fits) // chunk)
            table.append((count, chunk, before, end))
            low = top
    return table


def plan_kernel(coarse, table, *refs):
    parts = (len(refs) - 3) // 2
    lev_refs, (start_ref, which_ref), (*held, sems) = refs[:parts], refs[parts : parts + 2], refs[parts + 2 :]
    loads = [pltpu.make_async_copy(src, dst, sems.at[n]) for n, (src, dst) in enumerate(zip(lev_refs, held))]
    for load in loads:
        load.start()
    for load in loads:
        load.wait()
    lev_refs = held
    shared = []
    for b, y in GROUPS:
        holders = jnp.int32(0)
        for lev_ref in lev_refs:
            held = jnp.int32(0)
            for c in range(lev_ref.shape[0]):
                held = held | jnp.where((lev_ref[c, 0] >= b) & (lev_ref[c, 1] >= y), 1, 0)
            holders = holders + held
        shared.append(jnp.where(holders >= 2, 1, 0))
    sizes = group_sizes(coarse)
    counts, starts = [], []
    for part in sizes:
        count = jnp.int32(0)
        places = [jnp.int32(0)] * len(GROUPS)
        for wanted in (1, 0):
            for k, size in enumerate(part):
                take = shared[k] == wanted
                places[k] = jnp.where(take, count, places[k])
                count = count + jnp.where(take, size, 0)
            if wanted:
                counts.append(count)
        starts.append(places)
    total = counts[0] + counts[1]
    which = jnp.int32(0)
    ahead = jnp.int32(table[0][2] * table[0][1])
    for (count, size, _, _), (_, later, before, _) in zip(table, table[1:]):
        more = total > count * size
        which = which + jnp.where(more, 1, 0)
        ahead = jnp.where(more, before * later, ahead)
    which_ref[0] = which
    for k in range(len(GROUPS)):
        start_ref[k] = starts[0][k]
        start_ref[len(GROUPS) + k] = starts[1][k] + jnp.where(shared[k] == 1, ahead, sum(sizes[0]))
    start_ref[2 * len(GROUPS)] = ahead
    start_ref[2 * len(GROUPS) + 1] = counts[1]


def inner_slot(start_ref, group, offset):
    place = start_ref[group] + offset
    return place + jnp.where(place >= start_ref[2 * len(GROUPS)], start_ref[2 * len(GROUPS) + 1], 0)


def point_of(index, points):
    tier = jnp.where(index >= 4 * BASE, 4 * BASE, jnp.where(index >= 2 * BASE, 2 * BASE, BASE))
    step = jnp.where(index >= 4 * BASE, points >> 8, jnp.where(index >= 2 * BASE, points >> 7, points >> 6))
    fine = index >= BASE
    place = jnp.where(fine, (2 * (index - tier) + 1) * step, index * (points >> MINL))
    return place, jnp.where(fine, step, 0), fine


def halves(x):
    high = x.astype(jnp.bfloat16)
    return high, (x - high.astype(jnp.float32)).astype(jnp.bfloat16)


def dot(a, b, dims):
    return lax.dot_general(a, b, dims, preferred_element_type=jnp.float32)


def front_kernel(dom_shift, lev_ref, vel_ref, rate_ref, v_ref, s_ref, u_ref, first_ref, last_ref):
    g = pl.program_id(0)
    lx = lev_ref[g, 0]
    points = jnp.int32(1) << lx
    live = jnp.int32(1) << (lx + lev_ref[g, 1] - dom_shift)
    nu = vel_ref[g, 0] * points.astype(jnp.float32) / LINE
    centre = 1.0 - nu * nu
    ahead = 0.5 * nu * nu - 0.5 * nu
    behind = 0.5 * nu * nu + 0.5 * nu
    damp = 1.0 - TAU * rate_ref[g]
    p = lax.broadcasted_iota(jnp.int32, (LINE, LINE), 0)
    q = lax.broadcasted_iota(jnp.int32, (LINE, LINE), 1)
    wrap = points - 1
    place, step, fine = point_of(p & wrap, points)
    same = (p >> lx) == (q >> lx)
    off = ((q & wrap) - place) & wrap
    lower = (off + step) & wrap
    upper = (off - step) & wrap
    half = jnp.where(fine, -0.5, 0.0)

    def adv(d):
        return jnp.where(d == 0, centre, jnp.where(d == 1, ahead, jnp.where(d == wrap, behind, 0.0)))

    def one(d):
        return jnp.where(d == 0, 1.0, 0.0)

    mat_v = jnp.where(same, damp * (adv(off) + half * (adv(lower) + adv(upper))), 0.0)
    mat_hi, mat_lo = halves(mat_v)
    mat_s = jnp.where(same, TAU * (one(off) + half * (one(lower) + one(upper))), 0.0).astype(jnp.bfloat16)
    nt = (((1,), (1,)), ((), ()))
    last_block = jnp.maximum(live // LINE - 1, 0)

    def one_block(block, _):
        cut = pl.ds(pl.multiple_of(block * LINE, LINE), LINE)
        v_hi, v_lo = halves(v_ref[0, :, cut])
        s_hi, s_lo = halves(s_ref[0, :, cut])
        res = dot(mat_hi, v_hi, nt) + dot(mat_lo, v_hi, nt) + dot(mat_hi, v_lo, nt) + dot(mat_s, s_hi, nt) + dot(mat_s, s_lo, nt)
        u_ref[0, cut, :] = res

        @pl.when(block == 0)
        def _():
            first_ref[0] = res

        @pl.when(block == last_block)
        def _():
            last_ref[0] = res

        return 0

    lax.fori_loop(0, last_block + 1, one_block, 0)


def y_coefs(nu):
    return 1.0 - nu * nu, 0.5 * nu * nu - 0.5 * nu, 0.5 * nu * nu + 0.5 * nu


def group_of(tier, xu):
    band = jnp.where(xu >= 4, 3, jnp.where(xu >= 2, 2, xu))
    group = jnp.where(band == 0, tier, jnp.where(band == 1, 4 + tier, jnp.where(band == 2, 7 + tier, 9)))
    width = jnp.where(band >= 2, 1 << (band - 1), 1)
    return group, width, xu - jnp.where(band >= 2, width, band)


class Shape:
    def __init__(self, lev_ref, g, dom_shift):
        self.lx, self.ly = lev_ref[g, 0], lev_ref[g, 1]
        self.live = jnp.int32(1) << (self.lx + self.ly - dom_shift)
        self.units = self.live // BASE
        self.x_shift = self.lx - MINL
        self.nx = jnp.int32(1) << self.x_shift
        self.points = jnp.int32(1) << self.lx
        self.seg_shift = self.ly - MINL
        self.rows = self.units >> self.x_shift

    def tier(self, tier):
        step = jnp.int32(1) << (self.seg_shift - tier)
        fine = tier > 0
        count = jnp.where(fine, self.rows >> (self.seg_shift - tier + 1), self.rows >> self.seg_shift)
        return count, jnp.where(fine, step, 0), jnp.where(fine, step, 0), jnp.where(fine, 2 * step, step)


def add_surplus(t_ref, mov, shape, step, places, weight):
    away = step << shape.x_shift
    half = jnp.where(step > 0, 0.5, 0.0)
    sums = []
    for y, xu, slot in places:
        i = (y << shape.x_shift) + xu
        value = mov[rows_at(i), :] - half * (mov[rows_at(i - away), :] + mov[rows_at(i + away), :])
        sums.append(t_ref[rows_at(slot), :] + weight * value)
    for (_, _, slot), value in zip(places, sums):
        t_ref[rows_at(slot), :] = value


def clear(t_ref):
    def one(i, _):
        t_ref[rows_at(i), :] = jnp.zeros((BASE, t_ref.shape[1]), jnp.float32)
        return 0

    lax.fori_loop(0, t_ref.shape[0] // BASE, one, 0)


def send_out(t_ref, out_refs, sems):
    moves, at = [], 0
    for n, out_ref in enumerate(out_refs):
        size = out_ref.shape[0]
        moves.append(pltpu.make_async_copy(t_ref.at[at : at + size, :], out_ref, sems.at[n]))
        at += size
    for move in moves:
        move.start()
    for move in moves:
        move.wait()


def inner_kernel(dom_shift, n_out, lev_ref, vel_ref, coef_ref, start_ref, u_ref, *refs):
    out_refs, (t_ref, mov, sems) = refs[:n_out], refs[n_out:]
    clear(t_ref)

    def one_grid(g, _):
        shape = Shape(lev_ref, g, dom_shift)
        nx, x_shift = shape.nx, shape.x_shift
        centre, ahead, behind = y_coefs(vel_ref[g, 1] * (jnp.int32(1) << shape.ly).astype(jnp.float32) / LINE)
        weight = coef_ref[g].astype(jnp.float32)

        def step_y(n, _):
            i = nx + 2 * n
            mov[rows_at(i, 2), :] = (
                centre * u_ref[g, rows_at(i, 2), :] + ahead * u_ref[g, rows_at(i + nx, 2), :] + behind * u_ref[g, rows_at(i - nx, 2), :]
            )
            return 0

        lax.fori_loop(0, jnp.maximum(shape.units - 2 * nx, 0) >> 1, step_y, 0)

        def tier_loop(tier, _):
            count, step, first, stride = shape.tier(tier)

            def two(pair, _):
                places = []
                for n in (2 * pair, 2 * pair + 1):
                    j, xu = (n >> x_shift) + 1, n & (nx - 1)
                    group, width, place = group_of(tier, xu)
                    places.append((first + j * stride, xu, inner_slot(start_ref, group, (j - 1) * width + place)))
                add_surplus(t_ref, mov, shape, step, places, weight)
                return 0

            lax.fori_loop(0, (jnp.maximum(count - 2, 0) << x_shift) >> 1, two, 0)
            return 0

        lax.fori_loop(0, shape.seg_shift + 1, tier_loop, 0)
        return 0

    lax.fori_loop(0, u_ref.shape[0], one_grid, 0)
    send_out(t_ref, out_refs, sems)


def edge_kernel(dom_shift, n_out, sent, lev_ref, vel_ref, coef_ref, start_ref, u_ref, rest_ref, next_ref, prev_ref, *refs):
    out_refs, (t_ref, mov, sems) = refs[:n_out], refs[n_out:]
    load = pltpu.make_async_copy(rest_ref, t_ref, sems.at[n_out])
    load.start()
    halo_units = next_ref.shape[1] // BASE

    def one_grid(g, _):
        shape = Shape(lev_ref, g, dom_shift)
        nx, x_shift, units, rows = shape.nx, shape.x_shift, shape.units, shape.rows
        centre, ahead, behind = y_coefs(vel_ref[g, 1] * (jnp.int32(1) << shape.ly).astype(jnp.float32) / LINE)
        weight = coef_ref[g].astype(jnp.float32)
        prev_first = jnp.where(shape.live < LINE, units, halo_units) - nx

        def ends(xu, _):
            before = prev_ref[g, rows_at(prev_first + xu), :]
            head = u_ref[g, rows_at(xu), :]
            last = u_ref[g, rows_at(units - nx + xu), :]
            after = next_ref[g, rows_at(xu), :]

            @pl.when(rows == 1)
            def _():
                mov[rows_at(xu), :] = centre * head + ahead * after + behind * before

            @pl.when(rows > 1)
            def _():
                mov[rows_at(xu), :] = centre * head + ahead * u_ref[g, rows_at(nx + xu), :] + behind * before
                mov[rows_at(units - nx + xu), :] = centre * last + ahead * after + behind * u_ref[g, rows_at(units - 2 * nx + xu), :]

            @pl.when(shape.seg_shift > 0)
            def _():
                mov[rows_at(units + xu), :] = centre * after + ahead * next_ref[g, rows_at(nx + xu), :] + behind * last

            return 0

        lax.fori_loop(0, nx, ends, 0)

        def step_y(i, _):
            mov[rows_at(i), :] = centre * u_ref[g, rows_at(i), :] + ahead * u_ref[g, rows_at(i + nx), :] + behind * u_ref[g, rows_at(i - nx), :]
            return 0

        segment = jnp.int32(1) << shape.seg_shift
        near = jnp.minimum(segment, rows - 2)
        lax.fori_loop(nx, (near + 1) << x_shift, step_y, 0)
        lax.fori_loop(jnp.maximum(rows - segment, near + 1) << x_shift, (rows - 1) << x_shift, step_y, 0)

        @pl.when(g == 0)
        def _():
            load.wait()

        def tier_loop(tier, _):
            count, step, first, stride = shape.tier(tier)

            def one(n, _):
                end, xu = n >> x_shift, n & (nx - 1)
                group, width, place = group_of(tier, xu)
                slot = start_ref[len(GROUPS) + group] + end * width + place - sent
                add_surplus(t_ref, mov, shape, step, [(first + end * (count - 1) * stride, xu, slot)], weight)
                return 0

            lax.fori_loop(0, jnp.minimum(count, 2) << x_shift, one, 0)
            return 0

        lax.fori_loop(0, shape.seg_shift + 1, tier_loop, 0)
        return 0

    lax.fori_loop(0, u_ref.shape[0], one_grid, 0)
    send_out(t_ref, out_refs, sems)


def load_sums(t_ref, got, rest_ref, sems, first=0):
    count = lax.axis_size("grid")
    z = lax.axis_index("grid")
    passed_on = (z == 0) | (z == count - 1)
    at = 0
    waits = []
    for n, (total, passed) in enumerate(got):
        size = total.shape[0]
        dst = t_ref.at[at : at + size, :]
        if passed is None:
            pltpu.make_async_copy(total, dst, sems.at[n]).start()
        else:
            @pl.when(passed_on)
            def _():
                pltpu.make_async_copy(passed, dst, sems.at[n]).start()

            @pl.when(jnp.logical_not(passed_on))
            def _():
                pltpu.make_async_copy(total, dst, sems.at[n]).start()
        waits.append(pltpu.make_async_copy(total, dst, sems.at[n]))
        at += size
    if rest_ref is not None:
        at = t_ref.shape[0] - rest_ref.shape[0]
        waits.append(pltpu.make_async_copy(rest_ref, t_ref.at[at:, :], sems.at[len(got)]))
        waits[-1].start()
    for wait in waits:
        wait.wait()


def pairs_of(refs, count, paired):
    if paired:
        return [(refs[2 * n], refs[2 * n + 1]) for n in range(count)], refs[2 * count :]
    return [(refs[n], None) for n in range(count)], refs[count:]


def pack_kernel(coarse, sent, count, paired, has_rest, start_ref, *refs):
    got, refs = pairs_of(refs, count, paired)
    rest_ref, refs = (refs[0], refs[1:]) if has_rest else (None, refs)
    tail_ref, head_ref, t_ref, sems = refs
    load_sums(t_ref, got, rest_ref, sems)
    at = 0
    for k, (b, y) in enumerate(GROUPS):
        width = BAND_UNITS[b - MINL]
        last = start_ref[len(GROUPS) + k] + (region_units(y, coarse)[1] - 1) * width - sent
        tail_ref[at * BASE : (at + width) * BASE, :] = t_ref[rows_at(last, width), :]
        at += width
    at = 0
    for k in HEAD_GROUPS:
        width = BAND_UNITS[GROUPS[k][0] - MINL]
        head_ref[at * BASE : (at + width) * BASE, :] = t_ref[rows_at(start_ref[len(GROUPS) + k] - sent, width), :]
        at += width


def back_kernel(dom_shift, count, paired, has_rest, lev_ref, vel_ref, start_ref, tail_ref, head_ref, *refs):
    got, refs = pairs_of(refs, count, paired)
    rest_ref, refs = (refs[0], refs[1:]) if has_rest else (None, refs)
    out_ref, t_ref, val, comb, sems = refs
    g = pl.program_id(0)

    @pl.when(g == 0)
    def _():
        load_sums(t_ref, got, rest_ref, sems)

    shape = Shape(lev_ref, g, dom_shift)
    nx, x_shift, units, points, live, seg_shift, lx = shape.nx, shape.x_shift, shape.units, shape.points, shape.live, shape.seg_shift, shape.lx
    centre, ahead, behind = y_coefs(vel_ref[g, 1] * (jnp.int32(1) << shape.ly).astype(jnp.float32) / LINE)

    at_once = 2 if dom_shift < MINL else 1

    def gather_tier(tier, _):
        rows, step, first, stride = shape.tier(tier)

        def several(batch, _):
            moves = []
            for n in [batch * at_once + k for k in range(at_once)]:
                j, xu = n >> x_shift, n & (nx - 1)
                group, width, place = group_of(tier, xu)
                inside = inner_slot(start_ref, group, (j - 1) * width + place)
                outside = start_ref[len(GROUPS) + group] + jnp.where(j > 0, width, 0) + place
                slot = jnp.where((j > 0) & (j < rows - 1), inside, outside)
                moves.append((nx + ((first + j * stride) << x_shift) + xu, t_ref[rows_at(slot), :]))
            for i, row in moves:
                val[rows_at(i), :] = row
            return 0

        lax.fori_loop(0, (rows << x_shift) // at_once, several, 0)
        return 0

    lax.fori_loop(0, seg_shift + 1, gather_tier, 0)

    def edges(xu, _):
        after = val[rows_at(nx + xu), :]
        band = jnp.where(xu >= 4, 3, jnp.where(xu >= 2, 2, xu))
        width = jnp.where(band >= 2, 1 << (band - 1), 1)
        base = jnp.where(band == 0, 0, jnp.where(band == 1, 4 + xu - 1, jnp.where(band == 2, 7 + xu - 2, 11 + xu - 4)))

        def finer(tier, row):
            return tail_ref[rows_at(base + tier * width), :] + 0.5 * (row + after)

        val[rows_at(xu), :] = lax.fori_loop(1, seg_shift + 1, finer, tail_ref[rows_at(base), :])
        val[rows_at(nx + units + xu), :] = head_ref[rows_at(xu), :]
        return 0

    lax.fori_loop(0, nx, edges, 0)

    def tier_loop(tier, _):
        step_shift = seg_shift - tier
        away = jnp.int32(1) << (step_shift + x_shift)

        def lift(batch, _):
            lifted = []
            for j in [batch * at_once + k for k in range(at_once)]:
                y = ((j >> x_shift) * 2 + 1) << step_shift
                i = nx + (y << x_shift) + (j & (nx - 1))
                lifted.append((i, val[rows_at(i), :] + 0.5 * (val[rows_at(i - away), :] + val[rows_at(i + away), :])))
            for i, row in lifted:
                val[rows_at(i), :] = row
            return 0

        lax.fori_loop(0, (units >> (step_shift + 1)) // at_once, lift, 0)
        return 0

    lax.fori_loop(1, seg_shift + 1, tier_loop, 0)

    def step_y(i, _):
        i = 4 * i
        comb[rows_at(i, 4), :] = centre * val[rows_at(i + nx, 4), :] + ahead * val[rows_at(i + 2 * nx, 4), :] + behind * val[rows_at(i, 4), :]
        return 0

    lax.fori_loop(0, units >> 2, step_y, 0)

    def clear(i, _):
        comb[rows_at(i), :] = jnp.zeros((BASE, comb.shape[1]), jnp.float32)
        return 0

    lax.fori_loop(units, comb.shape[0] // BASE, clear, 0)

    p = lax.broadcasted_iota(jnp.int32, (LINE, LINE), 0)
    q = lax.broadcasted_iota(jnp.int32, (LINE, LINE), 1)
    wrap = points - 1
    place, step, fine = point_of(p & wrap, points)
    reach = jnp.where(fine, step, points >> MINL)
    inverse = jnp.where(fine, jnp.where(reach == 4, 0.25, jnp.where(reach == 2, 0.5, 1.0)), 1.0 / (points >> MINL).astype(jnp.float32))
    off = ((q & wrap) - place) & wrap
    apart = jnp.minimum(off, points - off)
    hat = jnp.maximum(0.0, 1.0 - apart.astype(jnp.float32) * inverse)
    mat = jnp.where((p >> lx) == (q >> lx), hat, 0.0)
    mat = mat.astype(jnp.bfloat16)
    tn = (((0,), (0,)), ((), ()))
    live_blocks = jnp.maximum(live // LINE, 1)

    def one_block(block, _):
        cut = pl.ds(pl.multiple_of(block * LINE, LINE), LINE)
        high, low = halves(comb[cut, :])
        out_ref[0, :, cut] = dot(high, mat, tn) + dot(low, mat, tn)
        return 0

    def no_block(block, _):
        out_ref[0, :, pl.ds(pl.multiple_of(block * LINE, LINE), LINE)] = jnp.zeros((out_ref.shape[1], LINE), jnp.float32)
        return 0

    lax.fori_loop(0, live_blocks, one_block, 0)
    lax.fori_loop(live_blocks, out_ref.shape[2] // LINE, no_block, 0)


def sum_line(parts):
    count = lax.axis_size("grid")
    if count == 1:
        return [(part, None) for part in parts]
    if count % 2:
        return [(lax.psum(part, "grid"), None) for part in parts]
    half = count // 2
    z = lax.axis_index("grid")
    at_end = (z == 0) | (z == count - 1)
    inwards = [(0, 1), (count - 1, count - 2)]
    outwards = [(1, 0), (count - 2, count - 1)]
    number = len(parts)
    arrived, held, crossed, done = {}, {}, {}, {}
    if half > 1:
        arrived = {n: lax.ppermute(parts[n], "grid", inwards) for n in range(min(AHEAD, number))}

    def finish(n):
        total = held[n] + crossed[n]
        for i in range(half - 2, 0, -1):
            came = lax.ppermute(total, "grid", [(i + 1, i), (count - 2 - i, count - 1 - i)])
            total = jnp.where((z == i) | (z == count - 1 - i), came, total)
        if half == 1:
            done[n] = (total, None)
        elif n + AHEAD < number:
            arrived[n + AHEAD] = lax.ppermute(jnp.where(at_end, parts[n + AHEAD], total), "grid", inwards + outwards)
            done[n] = (total, arrived[n + AHEAD])
        else:
            done[n] = (total, lax.ppermute(total, "grid", outwards))

    for n in range(number):
        total = parts[n]
        if half > 1:
            if n:
                arrived[n], held[n - 1] = lax.optimization_barrier((arrived[n], held[n - 1]))
            total = total + arrived[n]
        for i in range(1, half - 1):
            total = total + lax.ppermute(total, "grid", [(i, i + 1), (count - 1 - i, count - 2 - i)])
        held[n] = total
        crossed[n] = lax.ppermute(total, "grid", [(half - 1, half), (half, half - 1)])
        if n:
            crossed[n - 1], held[n] = lax.optimization_barrier((crossed[n - 1], held[n]))
            finish(n - 1)
    finish(number - 1)
    return [done[n] for n in range(number)]


SMEM = pl.BlockSpec(memory_space=pltpu.SMEM)
VMEM = pl.BlockSpec(memory_space=pltpu.VMEM)
ANY = pl.BlockSpec(memory_space=pl.ANY)


def per_grid(shape):
    return pl.BlockSpec((1,) + shape, lambda g: (g, 0, 0))


def run_branch(dom, sent, size, inner, end, operands):
    levels, velocity, comb_coefs, starts, values, first, last = operands
    f32 = jnp.float32
    grids, block_len, other = values.shape
    dom_shift = dom.bit_length() - 1
    coarse = BASE // dom
    chunk = size * BASE
    rest = TOTAL_UNITS * coarse * BASE - sent * chunk
    later = sent - inner
    params = pltpu.CompilerParams(vmem_limit_bytes=VMEM_BYTES)
    to_next = [(i, (i + 1) % dom) for i in range(dom)]
    to_prev = [(i, (i - 1) % dom) for i in range(dom)]

    def rows(n):
        return jax.ShapeDtypeStruct((n, other), f32)

    after = lax.ppermute(first, "dom", to_prev)
    before = lax.ppermute(last, "dom", to_next)

    outs = [rows(chunk)] * inner + [rows(later * chunk + rest)]
    *parts, held = pl.pallas_call(
        functools.partial(inner_kernel, dom_shift, len(outs)),
        in_specs=[SMEM] * 4 + [VMEM],
        out_specs=[ANY] * len(outs),
        out_shape=outs,
        scratch_shapes=[
            pltpu.VMEM((TOTAL_UNITS * coarse * BASE, other), f32),
            pltpu.VMEM((block_len + LINE, other), f32),
            pltpu.SemaphoreType.DMA((len(outs),)),
        ],
        compiler_params=params,
        name="inner",
    )(levels, velocity, comb_coefs, starts, values)

    outs = [rows(chunk)] * later + [rows(rest)] * (rest > 0)
    edges = list(pl.pallas_call(
        functools.partial(edge_kernel, dom_shift, len(outs), inner * chunk // BASE),
        in_specs=[SMEM] * 4 + [VMEM, ANY, VMEM, VMEM],
        out_specs=[ANY] * len(outs),
        out_shape=outs,
        scratch_shapes=[
            pltpu.VMEM((later * chunk + rest, other), f32),
            pltpu.VMEM((block_len + LINE, other), f32),
            pltpu.SemaphoreType.DMA((len(outs) + 1,)),
        ],
        compiler_params=params,
        name="edge",
    )(levels, velocity, comb_coefs, starts, values, held, after, before))
    own = edges[later:]
    parts = parts + edges[:later]

    summed = sum_line(parts)
    paired = summed[0][1] is not None
    flat = [x for n in range(sent) for x in summed[n] if x is not None]
    flat_later = [x for n in range(inner, end) for x in summed[n] if x is not None]

    tail_rows = sum(BAND_UNITS[b - MINL] for b, _ in GROUPS) * BASE
    head_rows = sum(BAND_UNITS) * BASE
    tail, head = pl.pallas_call(
        functools.partial(pack_kernel, coarse, inner * size, end - inner, paired, rest > 0),
        in_specs=[SMEM] + [ANY] * (len(flat_later) + len(own)),
        out_specs=[VMEM, VMEM],
        out_shape=[rows(tail_rows), rows(head_rows)],
        scratch_shapes=[pltpu.VMEM((later * chunk + rest, other), f32), pltpu.SemaphoreType.DMA((end - inner + 1,))],
        compiler_params=params,
        name="pack",
    )(starts, *flat_later, *own)
    tail = lax.ppermute(tail, "dom", to_next)
    head = lax.ppermute(head, "dom", to_prev)

    return pl.pallas_call(
        functools.partial(back_kernel, dom_shift, sent, paired, rest > 0),
        grid=(grids,),
        in_specs=[SMEM] * 3 + [VMEM, VMEM] + [ANY] * (len(flat) + len(own)),
        out_specs=per_grid((other, block_len)),
        out_shape=jax.ShapeDtypeStruct((grids, other, block_len), f32),
        scratch_shapes=[
            pltpu.VMEM((sent * chunk + rest, other), f32),
            pltpu.VMEM((block_len + 2 * LINE, other), f32),
            pltpu.VMEM((block_len, other), f32),
            pltpu.SemaphoreType.DMA((sent + 1,)),
        ],
        compiler_params=pltpu.CompilerParams(vmem_limit_bytes=VMEM_BYTES),
        name="back",
    )(levels, velocity, starts, tail, head, *flat, *own)


def local(nodal_values, source_term, velocity, react_rate, levels, comb_coefs):
    grids, other, block_len = nodal_values.shape
    dom = lax.axis_size("dom")
    count = lax.axis_size("grid")
    dom_shift = dom.bit_length() - 1
    coarse = BASE // dom
    f32 = jnp.float32
    all_levels = [levels] + [lax.ppermute(levels, "grid", [(i, (i + k) % count) for i in range(count)]) for k in range(1, count)]

    values, first, last = pl.pallas_call(
        functools.partial(front_kernel, dom_shift),
        grid=(grids,),
        in_specs=[SMEM, SMEM, SMEM, per_grid((other, block_len)), per_grid((other, block_len))],
        out_specs=[per_grid((block_len, other)), per_grid((LINE, other)), per_grid((LINE, other))],
        out_shape=[
            jax.ShapeDtypeStruct((grids, block_len, other), f32),
            jax.ShapeDtypeStruct((grids, LINE, other), f32),
            jax.ShapeDtypeStruct((grids, LINE, other), f32),
        ],
        compiler_params=pltpu.CompilerParams(vmem_limit_bytes=VMEM_MOST),
        name="front",
    )(levels, velocity, react_rate, nodal_values, source_term)

    table = branch_table(coarse)
    starts, which = pl.pallas_call(
        functools.partial(plan_kernel, coarse, table),
        in_specs=[ANY] * count,
        out_specs=[SMEM, SMEM],
        scratch_shapes=[pltpu.SMEM(levels.shape, jnp.int32)] * count + [pltpu.SemaphoreType.DMA((count,))],
        out_shape=[jax.ShapeDtypeStruct((2 * len(GROUPS) + 2,), jnp.int32), jax.ShapeDtypeStruct((1,), jnp.int32)],
        name="plan",
    )(*all_levels)

    operands = (levels, velocity, comb_coefs, starts, values, first, last)
    branches = [functools.partial(run_branch, dom, *row) for row in table]
    return lax.switch(which[0], branches, operands)


def solution(mesh):
    in_specs = (
        P("grid", None, "dom"),
        P("grid", None, "dom"),
        P("grid", None),
        P("grid"),
        P("grid", None),
        P("grid"),
    )
    return jax.shard_map(local, mesh=mesh, in_specs=in_specs, out_specs=P("grid", None, "dom"), check_vma=False)
```

```python
import functools
import itertools

import jax
import jax.numpy as jnp
from jax import lax
from jax.experimental import pallas as pl
from jax.experimental.pallas import tpu as pltpu
from jax.sharding import PartitionSpec as P

MAXL = 8
MINL = 5
LSUM = 13
LINE = 2**MAXL
BASE = 2**MINL
TAU = 0.25
VMEM_BYTES = 48 * 2**20
VMEM_MOST = 63 * 2**20
BRANCHES = [(6, 3), (7, 4), (8, 4), (10, 5), (11, 4), (12, 4), (14, 5)]
AHEAD = 3
EARLY = 1

GROUPS = [(b, y) for b in range(MINL, MAXL + 1) for y in range(MINL, LSUM - b + 1)]
BAND_UNITS = [1] + [2**t for t in range(MAXL - MINL)]
BAND_FIRST = [0] + [2**t for t in range(MAXL - MINL)]


def group_rows(y):
    return 1 if y == MINL else 2 ** (y - MINL - 1)


GROUP_UNITS = [group_rows(y) * BAND_UNITS[b - MINL] for b, y in GROUPS]
TOTAL_UNITS = sum(GROUP_UNITS)
HEAD_GROUPS = [k for k, (b, y) in enumerate(GROUPS) if y == MINL]


def rows_at(unit, count=1):
    return pl.ds(pl.multiple_of(unit * BASE, BASE), count * BASE)


def region_units(y, coarse):
    rows = group_rows(y) * coarse
    return max(rows - 2, 0), min(rows, 2)


def group_sizes(coarse):
    inner, edge = zip(*[region_units(y, coarse) for _, y in GROUPS])
    widths = [BAND_UNITS[b - MINL] for b, _ in GROUPS]
    return [n * w for n, w in zip(inner, widths)], [n * w for n, w in zip(edge, widths)]


def branch_table(coarse):
    inner, edge = group_sizes(coarse)
    tops = [[-1] + list(range(MINL, LSUM - b + 1)) for b in range(MINL, MAXL + 1)]
    cases = []
    for top in itertools.product(*tops):
        if all(hi >= lo for hi, lo in zip(top, top[1:])):
            held = [y <= top[b - MINL] for b, y in GROUPS]
            cases.append((sum(n for n, h in zip(inner, held) if h), sum(n for n, h in zip(edge, held) if h)))
    table, low = [], -1
    for size, count in BRANCHES + [(TOTAL_UNITS, 5)]:
        chunk = -(-size * coarse // count)
        top = count * chunk
        fits = [(i, e) for i, e in cases if low < i + e <= top]
        if fits:
            before = min(min(i for i, _ in fits) // chunk, EARLY)
            spill = any(top > sum(inner) + e and e < sum(edge) for _, e in fits)
            end = count if spill else before - (-max(e for _, e in fits) // chunk)
            table.append((count, chunk, before, end))
            low = top
    return table


def plan_kernel(coarse, table, *refs):
    parts = (len(refs) - 3) // 2
    lev_refs, (start_ref, which_ref), (*held, sems) = refs[:parts], refs[parts : parts + 2], refs[parts + 2 :]
    loads = [pltpu.make_async_copy(src, dst, sems.at[n]) for n, (src, dst) in enumerate(zip(lev_refs, held))]
    for load in loads:
        load.start()
    for load in loads:
        load.wait()
    lev_refs = held
    shared = []
    for b, y in GROUPS:
        holders = jnp.int32(0)
        for lev_ref in lev_refs:
            held = jnp.int32(0)
            for c in range(lev_ref.shape[0]):
                held = held | jnp.where((lev_ref[c, 0] >= b) & (lev_ref[c, 1] >= y), 1, 0)
            holders = holders + held
        shared.append(jnp.where(holders >= 2, 1, 0))
    sizes = group_sizes(coarse)
    counts, starts = [], []
    for part in sizes:
        count = jnp.int32(0)
        places = [jnp.int32(0)] * len(GROUPS)
        for wanted in (1, 0):
            for k, size in enumerate(part):
                take = shared[k] == wanted
                places[k] = jnp.where(take, count, places[k])
                count = count + jnp.where(take, size, 0)
            if wanted:
                counts.append(count)
        starts.append(places)
    total = counts[0] + counts[1]
    which = jnp.int32(0)
    ahead = jnp.int32(table[0][2] * table[0][1])
    for (count, size, _, _), (_, later, before, _) in zip(table, table[1:]):
        more = total > count * size
        which = which + jnp.where(more, 1, 0)
        ahead = jnp.where(more, before * later, ahead)
    which_ref[0] = which
    for k in range(len(GROUPS)):
        start_ref[k] = starts[0][k]
        start_ref[len(GROUPS) + k] = starts[1][k] + jnp.where(shared[k] == 1, ahead, sum(sizes[0]))
    start_ref[2 * len(GROUPS)] = ahead
    start_ref[2 * len(GROUPS) + 1] = counts[1]


def inner_slot(start_ref, group, offset):
    place = start_ref[group] + offset
    return place + jnp.where(place >= start_ref[2 * len(GROUPS)], start_ref[2 * len(GROUPS) + 1], 0)


def point_of(index, points):
    tier = jnp.where(index >= 4 * BASE, 4 * BASE, jnp.where(index >= 2 * BASE, 2 * BASE, BASE))
    step = jnp.where(index >= 4 * BASE, points >> 8, jnp.where(index >= 2 * BASE, points >> 7, points >> 6))
    fine = index >= BASE
    place = jnp.where(fine, (2 * (index - tier) + 1) * step, index * (points >> MINL))
    return place, jnp.where(fine, step, 0), fine


def halves(x):
    high = x.astype(jnp.bfloat16)
    return high, (x - high.astype(jnp.float32)).astype(jnp.bfloat16)


def dot(a, b, dims):
    return lax.dot_general(a, b, dims, preferred_element_type=jnp.float32)


def front_kernel(dom_shift, lev_ref, vel_ref, rate_ref, v_ref, s_ref, u_ref, first_ref, last_ref):
    g = pl.program_id(0)
    lx = lev_ref[g, 0]
    points = jnp.int32(1) << lx
    live = jnp.int32(1) << (lx + lev_ref[g, 1] - dom_shift)
    nu = vel_ref[g, 0] * points.astype(jnp.float32) / LINE
    centre = 1.0 - nu * nu
    ahead = 0.5 * nu * nu - 0.5 * nu
    behind = 0.5 * nu * nu + 0.5 * nu
    damp = 1.0 - TAU * rate_ref[g]
    p = lax.broadcasted_iota(jnp.int32, (LINE, LINE), 0)
    q = lax.broadcasted_iota(jnp.int32, (LINE, LINE), 1)
    wrap = points - 1
    place, step, fine = point_of(p & wrap, points)
    same = (p >> lx) == (q >> lx)
    off = ((q & wrap) - place) & wrap
    lower = (off + step) & wrap
    upper = (off - step) & wrap
    half = jnp.where(fine, -0.5, 0.0)

    def adv(d):
        return jnp.where(d == 0, centre, jnp.where(d == 1, ahead, jnp.where(d == wrap, behind, 0.0)))

    def one(d):
        return jnp.where(d == 0, 1.0, 0.0)

    mat_v = jnp.where(same, damp * (adv(off) + half * (adv(lower) + adv(upper))), 0.0)
    mat_hi, mat_lo = halves(mat_v)
    mat_s = jnp.where(same, TAU * (one(off) + half * (one(lower) + one(upper))), 0.0).astype(jnp.bfloat16)
    nt = (((1,), (1,)), ((), ()))
    last_block = jnp.maximum(live // LINE - 1, 0)

    def one_block(block, _):
        cut = pl.ds(pl.multiple_of(block * LINE, LINE), LINE)
        v_hi, v_lo = halves(v_ref[0, :, cut])
        s_hi, s_lo = halves(s_ref[0, :, cut])
        res = dot(mat_hi, v_hi, nt) + dot(mat_lo, v_hi, nt) + dot(mat_hi, v_lo, nt) + dot(mat_s, s_hi, nt) + dot(mat_s, s_lo, nt)
        u_ref[0, cut, :] = res

        @pl.when(block == 0)
        def _():
            first_ref[0] = res

        @pl.when(block == last_block)
        def _():
            last_ref[0] = res

        return 0

    lax.fori_loop(0, last_block + 1, one_block, 0)


def y_coefs(nu):
    return 1.0 - nu * nu, 0.5 * nu * nu - 0.5 * nu, 0.5 * nu * nu + 0.5 * nu


def group_of(tier, xu):
    band = jnp.where(xu >= 4, 3, jnp.where(xu >= 2, 2, xu))
    group = jnp.where(band == 0, tier, jnp.where(band == 1, 4 + tier, jnp.where(band == 2, 7 + tier, 9)))
    width = jnp.where(band >= 2, 1 << (band - 1), 1)
    return group, width, xu - jnp.where(band >= 2, width, band)


class Shape:
    def __init__(self, lev_ref, g, dom_shift):
        self.lx, self.ly = lev_ref[g, 0], lev_ref[g, 1]
        self.live = jnp.int32(1) << (self.lx + self.ly - dom_shift)
        self.units = self.live // BASE
        self.x_shift = self.lx - MINL
        self.nx = jnp.int32(1) << self.x_shift
        self.points = jnp.int32(1) << self.lx
        self.seg_shift = self.ly - MINL
        self.rows = self.units >> self.x_shift

    def tier(self, tier):
        step = jnp.int32(1) << (self.seg_shift - tier)
        fine = tier > 0
        count = jnp.where(fine, self.rows >> (self.seg_shift - tier + 1), self.rows >> self.seg_shift)
        return count, jnp.where(fine, step, 0), jnp.where(fine, step, 0), jnp.where(fine, 2 * step, step)


def add_surplus(t_ref, mov, shape, step, places, weight):
    away = step << shape.x_shift
    half = jnp.where(step > 0, 0.5, 0.0)
    sums = []
    for y, xu, slot in places:
        i = (y << shape.x_shift) + xu
        value = mov[rows_at(i), :] - half * (mov[rows_at(i - away), :] + mov[rows_at(i + away), :])
        sums.append(t_ref[rows_at(slot), :] + weight * value)
    for (_, _, slot), value in zip(places, sums):
        t_ref[rows_at(slot), :] = value


def clear(t_ref):
    def one(i, _):
        t_ref[rows_at(i), :] = jnp.zeros((BASE, t_ref.shape[1]), jnp.float32)
        return 0

    lax.fori_loop(0, t_ref.shape[0] // BASE, one, 0)


def send_out(t_ref, out_refs, sems):
    moves, at = [], 0
    for n, out_ref in enumerate(out_refs):
        size = out_ref.shape[0]
        moves.append(pltpu.make_async_copy(t_ref.at[at : at + size, :], out_ref, sems.at[n]))
        at += size
    for move in moves:
        move.start()
    for move in moves:
        move.wait()


def inner_kernel(dom_shift, n_out, lev_ref, vel_ref, coef_ref, start_ref, u_ref, *refs):
    out_refs, (t_ref, mov, sems) = refs[:n_out], refs[n_out:]
    clear(t_ref)

    def one_grid(g, _):
        shape = Shape(lev_ref, g, dom_shift)
        nx, x_shift = shape.nx, shape.x_shift
        centre, ahead, behind = y_coefs(vel_ref[g, 1] * (jnp.int32(1) << shape.ly).astype(jnp.float32) / LINE)
        weight = coef_ref[g].astype(jnp.float32)

        def step_y(n, _):
            i = nx + 2 * n
            mov[rows_at(i, 2), :] = (
                centre * u_ref[g, rows_at(i, 2), :] + ahead * u_ref[g, rows_at(i + nx, 2), :] + behind * u_ref[g, rows_at(i - nx, 2), :]
            )
            return 0

        lax.fori_loop(0, jnp.maximum(shape.units - 2 * nx, 0) >> 1, step_y, 0)

        def tier_loop(tier, _):
            count, step, first, stride = shape.tier(tier)

            def two(pair, _):
                places = []
                for n in (2 * pair, 2 * pair + 1):
                    j, xu = (n >> x_shift) + 1, n & (nx - 1)
                    group, width, place = group_of(tier, xu)
                    places.append((first + j * stride, xu, inner_slot(start_ref, group, (j - 1) * width + place)))
                add_surplus(t_ref, mov, shape, step, places, weight)
                return 0

            lax.fori_loop(0, (jnp.maximum(count - 2, 0) << x_shift) >> 1, two, 0)
            return 0

        lax.fori_loop(0, shape.seg_shift + 1, tier_loop, 0)
        return 0

    lax.fori_loop(0, u_ref.shape[0], one_grid, 0)
    send_out(t_ref, out_refs, sems)


def edge_kernel(dom_shift, n_out, sent, lev_ref, vel_ref, coef_ref, start_ref, u_ref, rest_ref, next_ref, prev_ref, *refs):
    out_refs, (t_ref, mov, sems) = refs[:n_out], refs[n_out:]
    load = pltpu.make_async_copy(rest_ref, t_ref, sems.at[n_out])
    load.start()
    halo_units = next_ref.shape[1] // BASE

    def one_grid(g, _):
        shape = Shape(lev_ref, g, dom_shift)
        nx, x_shift, units, rows = shape.nx, shape.x_shift, shape.units, shape.rows
        centre, ahead, behind = y_coefs(vel_ref[g, 1] * (jnp.int32(1) << shape.ly).astype(jnp.float32) / LINE)
        weight = coef_ref[g].astype(jnp.float32)
        prev_first = jnp.where(shape.live < LINE, units, halo_units) - nx

        def ends(xu, _):
            before = prev_ref[g, rows_at(prev_first + xu), :]
            head = u_ref[g, rows_at(xu), :]
            last = u_ref[g, rows_at(units - nx + xu), :]
            after = next_ref[g, rows_at(xu), :]

            @pl.when(rows == 1)
            def _():
                mov[rows_at(xu), :] = centre * head + ahead * after + behind * before

            @pl.when(rows > 1)
            def _():
                mov[rows_at(xu), :] = centre * head + ahead * u_ref[g, rows_at(nx + xu), :] + behind * before
                mov[rows_at(units - nx + xu), :] = centre * last + ahead * after + behind * u_ref[g, rows_at(units - 2 * nx + xu), :]

            @pl.when(shape.seg_shift > 0)
            def _():
                mov[rows_at(units + xu), :] = centre * after + ahead * next_ref[g, rows_at(nx + xu), :] + behind * last

            return 0

        lax.fori_loop(0, nx, ends, 0)

        def step_y(i, _):
            mov[rows_at(i), :] = centre * u_ref[g, rows_at(i), :] + ahead * u_ref[g, rows_at(i + nx), :] + behind * u_ref[g, rows_at(i - nx), :]
            return 0

        segment = jnp.int32(1) << shape.seg_shift
        near = jnp.minimum(segment, rows - 2)
        lax.fori_loop(nx, (near + 1) << x_shift, step_y, 0)
        lax.fori_loop(jnp.maximum(rows - segment, near + 1) << x_shift, (rows - 1) << x_shift, step_y, 0)

        @pl.when(g == 0)
        def _():
            load.wait()

        def tier_loop(tier, _):
            count, step, first, stride = shape.tier(tier)

            def one(n, _):
                end, xu = n >> x_shift, n & (nx - 1)
                group, width, place = group_of(tier, xu)
                slot = start_ref[len(GROUPS) + group] + end * width + place - sent
                add_surplus(t_ref, mov, shape, step, [(first + end * (count - 1) * stride, xu, slot)], weight)
                return 0

            lax.fori_loop(0, jnp.minimum(count, 2) << x_shift, one, 0)
            return 0

        lax.fori_loop(0, shape.seg_shift + 1, tier_loop, 0)
        return 0

    lax.fori_loop(0, u_ref.shape[0], one_grid, 0)
    send_out(t_ref, out_refs, sems)


def load_sums(t_ref, got, rest_ref, sems, first=0):
    count = lax.axis_size("grid")
    z = lax.axis_index("grid")
    passed_on = (z == 0) | (z == count - 1)
    at = 0
    waits = []
    for n, (total, passed) in enumerate(got):
        size = total.shape[0]
        dst = t_ref.at[at : at + size, :]
        if passed is None:
            pltpu.make_async_copy(total, dst, sems.at[n]).start()
        else:
            @pl.when(passed_on)
            def _():
                pltpu.make_async_copy(passed, dst, sems.at[n]).start()

            @pl.when(jnp.logical_not(passed_on))
            def _():
                pltpu.make_async_copy(total, dst, sems.at[n]).start()
        waits.append(pltpu.make_async_copy(total, dst, sems.at[n]))
        at += size
    if rest_ref is not None:
        at = t_ref.shape[0] - rest_ref.shape[0]
        waits.append(pltpu.make_async_copy(rest_ref, t_ref.at[at:, :], sems.at[len(got)]))
        waits[-1].start()
    for wait in waits:
        wait.wait()


def pairs_of(refs, count, paired):
    if paired:
        return [(refs[2 * n], refs[2 * n + 1]) for n in range(count)], refs[2 * count :]
    return [(refs[n], None) for n in range(count)], refs[count:]


def pack_kernel(coarse, sent, count, paired, has_rest, start_ref, *refs):
    got, refs = pairs_of(refs, count, paired)
    rest_ref, refs = (refs[0], refs[1:]) if has_rest else (None, refs)
    tail_ref, head_ref, t_ref, sems = refs
    load_sums(t_ref, got, rest_ref, sems)
    at = 0
    for k, (b, y) in enumerate(GROUPS):
        width = BAND_UNITS[b - MINL]
        last = start_ref[len(GROUPS) + k] + (region_units(y, coarse)[1] - 1) * width - sent
        tail_ref[at * BASE : (at + width) * BASE, :] = t_ref[rows_at(last, width), :]
        at += width
    at = 0
    for k in HEAD_GROUPS:
        width = BAND_UNITS[GROUPS[k][0] - MINL]
        head_ref[at * BASE : (at + width) * BASE, :] = t_ref[rows_at(start_ref[len(GROUPS) + k] - sent, width), :]
        at += width


def back_kernel(dom_shift, count, paired, has_rest, lev_ref, vel_ref, start_ref, tail_ref, head_ref, *refs):
    got, refs = pairs_of(refs, count, paired)
    rest_ref, refs = (refs[0], refs[1:]) if has_rest else (None, refs)
    out_ref, t_ref, val, comb, sems = refs
    g = pl.program_id(0)

    @pl.when(g == 0)
    def _():
        load_sums(t_ref, got, rest_ref, sems)

    shape = Shape(lev_ref, g, dom_shift)
    nx, x_shift, units, points, live, seg_shift, lx = shape.nx, shape.x_shift, shape.units, shape.points, shape.live, shape.seg_shift, shape.lx
    centre, ahead, behind = y_coefs(vel_ref[g, 1] * (jnp.int32(1) << shape.ly).astype(jnp.float32) / LINE)

    at_once = 2 if dom_shift < MINL else 1

    def gather_tier(tier, _):
        rows, step, first, stride = shape.tier(tier)

        def several(batch, _):
            moves = []
            for n in [batch * at_once + k for k in range(at_once)]:
                j, xu = n >> x_shift, n & (nx - 1)
                group, width, place = group_of(tier, xu)
                inside = inner_slot(start_ref, group, (j - 1) * width + place)
                outside = start_ref[len(GROUPS) + group] + jnp.where(j > 0, width, 0) + place
                slot = jnp.where((j > 0) & (j < rows - 1), inside, outside)
                moves.append((nx + ((first + j * stride) << x_shift) + xu, t_ref[rows_at(slot), :]))
            for i, row in moves:
                val[rows_at(i), :] = row
            return 0

        lax.fori_loop(0, (rows << x_shift) // at_once, several, 0)
        return 0

    lax.fori_loop(0, seg_shift + 1, gather_tier, 0)

    def edges(xu, _):
        after = val[rows_at(nx + xu), :]
        band = jnp.where(xu >= 4, 3, jnp.where(xu >= 2, 2, xu))
        width = jnp.where(band >= 2, 1 << (band - 1), 1)
        base = jnp.where(band == 0, 0, jnp.where(band == 1, 4 + xu - 1, jnp.where(band == 2, 7 + xu - 2, 11 + xu - 4)))

        def finer(tier, row):
            return tail_ref[rows_at(base + tier * width), :] + 0.5 * (row + after)

        val[rows_at(xu), :] = lax.fori_loop(1, seg_shift + 1, finer, tail_ref[rows_at(base), :])
        val[rows_at(nx + units + xu), :] = head_ref[rows_at(xu), :]
        return 0

    lax.fori_loop(0, nx, edges, 0)

    def tier_loop(tier, _):
        step_shift = seg_shift - tier
        away = jnp.int32(1) << (step_shift + x_shift)

        def lift(batch, _):
            lifted = []
            for j in [batch * at_once + k for k in range(at_once)]:
                y = ((j >> x_shift) * 2 + 1) << step_shift
                i = nx + (y << x_shift) + (j & (nx - 1))
                lifted.append((i, val[rows_at(i), :] + 0.5 * (val[rows_at(i - away), :] + val[rows_at(i + away), :])))
            for i, row in lifted:
                val[rows_at(i), :] = row
            return 0

        lax.fori_loop(0, (units >> (step_shift + 1)) // at_once, lift, 0)
        return 0

    lax.fori_loop(1, seg_shift + 1, tier_loop, 0)

    def step_y(i, _):
        i = 4 * i
        comb[rows_at(i, 4), :] = centre * val[rows_at(i + nx, 4), :] + ahead * val[rows_at(i + 2 * nx, 4), :] + behind * val[rows_at(i, 4), :]
        return 0

    lax.fori_loop(0, units >> 2, step_y, 0)

    def clear(i, _):
        comb[rows_at(i), :] = jnp.zeros((BASE, comb.shape[1]), jnp.float32)
        return 0

    lax.fori_loop(units, comb.shape[0] // BASE, clear, 0)

    p = lax.broadcasted_iota(jnp.int32, (LINE, LINE), 0)
    q = lax.broadcasted_iota(jnp.int32, (LINE, LINE), 1)
    wrap = points - 1
    place, step, fine = point_of(p & wrap, points)
    reach = jnp.where(fine, step, points >> MINL)
    inverse = jnp.where(fine, jnp.where(reach == 4, 0.25, jnp.where(reach == 2, 0.5, 1.0)), 1.0 / (points >> MINL).astype(jnp.float32))
    off = ((q & wrap) - place) & wrap
    apart = jnp.minimum(off, points - off)
    hat = jnp.maximum(0.0, 1.0 - apart.astype(jnp.float32) * inverse)
    mat = jnp.where((p >> lx) == (q >> lx), hat, 0.0)
    mat = mat.astype(jnp.bfloat16)
    tn = (((0,), (0,)), ((), ()))
    live_blocks = jnp.maximum(live // LINE, 1)

    def one_block(block, _):
        cut = pl.ds(pl.multiple_of(block * LINE, LINE), LINE)
        high, low = halves(comb[cut, :])
        out_ref[0, :, cut] = dot(high, mat, tn) + dot(low, mat, tn)
        return 0

    def no_block(block, _):
        out_ref[0, :, pl.ds(pl.multiple_of(block * LINE, LINE), LINE)] = jnp.zeros((out_ref.shape[1], LINE), jnp.float32)
        return 0

    lax.fori_loop(0, live_blocks, one_block, 0)
    lax.fori_loop(live_blocks, out_ref.shape[2] // LINE, no_block, 0)


def sum_line(parts):
    count = lax.axis_size("grid")
    if count == 1:
        return [(part, None) for part in parts]
    if count % 2:
        return [(lax.psum(part, "grid"), None) for part in parts]
    half = count // 2
    z = lax.axis_index("grid")
    at_end = (z == 0) | (z == count - 1)
    inwards = [(0, 1), (count - 1, count - 2)]
    outwards = [(1, 0), (count - 2, count - 1)]
    number = len(parts)
    arrived, held, crossed, done = {}, {}, {}, {}
    if half > 1:
        arrived = {n: lax.ppermute(parts[n], "grid", inwards) for n in range(min(AHEAD, number))}

    def finish(n):
        total = held[n] + crossed[n]
        for i in range(half - 2, 0, -1):
            came = lax.ppermute(total, "grid", [(i + 1, i), (count - 2 - i, count - 1 - i)])
            total = jnp.where((z == i) | (z == count - 1 - i), came, total)
        if half == 1:
            done[n] = (total, None)
        elif n + AHEAD < number:
            arrived[n + AHEAD] = lax.ppermute(jnp.where(at_end, parts[n + AHEAD], total), "grid", inwards + outwards)
            done[n] = (total, arrived[n + AHEAD])
        else:
            done[n] = (total, lax.ppermute(total, "grid", outwards))

    for n in range(number):
        total = parts[n]
        if half > 1:
            if n:
                arrived[n], held[n - 1] = lax.optimization_barrier((arrived[n], held[n - 1]))
            total = total + arrived[n]
        for i in range(1, half - 1):
            total = total + lax.ppermute(total, "grid", [(i, i + 1), (count - 1 - i, count - 2 - i)])
        held[n] = total
        crossed[n] = lax.ppermute(total, "grid", [(half - 1, half), (half, half - 1)])
        if n:
            crossed[n - 1], held[n] = lax.optimization_barrier((crossed[n - 1], held[n]))
            finish(n - 1)
    finish(number - 1)
    return [done[n] for n in range(number)]


SMEM = pl.BlockSpec(memory_space=pltpu.SMEM)
VMEM = pl.BlockSpec(memory_space=pltpu.VMEM)
ANY = pl.BlockSpec(memory_space=pl.ANY)


def per_grid(shape):
    return pl.BlockSpec((1,) + shape, lambda g: (g, 0, 0))


def run_branch(dom, sent, size, inner, end, operands):
    levels, velocity, comb_coefs, starts, values, first, last = operands
    f32 = jnp.float32
    grids, block_len, other = values.shape
    dom_shift = dom.bit_length() - 1
    coarse = BASE // dom
    chunk = size * BASE
    rest = TOTAL_UNITS * coarse * BASE - sent * chunk
    later = sent - inner
    params = pltpu.CompilerParams(vmem_limit_bytes=VMEM_BYTES)
    to_next = [(i, (i + 1) % dom) for i in range(dom)]
    to_prev = [(i, (i - 1) % dom) for i in range(dom)]

    def rows(n):
        return jax.ShapeDtypeStruct((n, other), f32)

    after = lax.ppermute(first, "dom", to_prev)
    before = lax.ppermute(last, "dom", to_next)

    outs = [rows(chunk)] * inner + [rows(later * chunk + rest)]
    *parts, held = pl.pallas_call(
        functools.partial(inner_kernel, dom_shift, len(outs)),
        in_specs=[SMEM] * 4 + [VMEM],
        out_specs=[ANY] * len(outs),
        out_shape=outs,
        scratch_shapes=[
            pltpu.VMEM((TOTAL_UNITS * coarse * BASE, other), f32),
            pltpu.VMEM((block_len + LINE, other), f32),
            pltpu.SemaphoreType.DMA((len(outs),)),
        ],
        compiler_params=params,
        name="inner",
    )(levels, velocity, comb_coefs, starts, values)

    outs = [rows(chunk)] * later + [rows(rest)] * (rest > 0)
    edges = list(pl.pallas_call(
        functools.partial(edge_kernel, dom_shift, len(outs), inner * chunk // BASE),
        in_specs=[SMEM] * 4 + [VMEM, ANY, VMEM, VMEM],
        out_specs=[ANY] * len(outs),
        out_shape=outs,
        scratch_shapes=[
            pltpu.VMEM((later * chunk + rest, other), f32),
            pltpu.VMEM((block_len + LINE, other), f32),
            pltpu.SemaphoreType.DMA((len(outs) + 1,)),
        ],
        compiler_params=params,
        name="edge",
    )(levels, velocity, comb_coefs, starts, values, held, after, before))
    own = edges[later:]
    parts = parts + edges[:later]

    summed = sum_line(parts)
    paired = summed[0][1] is not None
    flat = [x for n in range(sent) for x in summed[n] if x is not None]
    flat_later = [x for n in range(inner, end) for x in summed[n] if x is not None]

    tail_rows = sum(BAND_UNITS[b - MINL] for b, _ in GROUPS) * BASE
    head_rows = sum(BAND_UNITS) * BASE
    tail, head = pl.pallas_call(
        functools.partial(pack_kernel, coarse, inner * size, end - inner, paired, rest > 0),
        in_specs=[SMEM] + [ANY] * (len(flat_later) + len(own)),
        out_specs=[VMEM, VMEM],
        out_shape=[rows(tail_rows), rows(head_rows)],
        scratch_shapes=[pltpu.VMEM((later * chunk + rest, other), f32), pltpu.SemaphoreType.DMA((end - inner + 1,))],
        compiler_params=params,
        name="pack",
    )(starts, *flat_later, *own)
    tail = lax.ppermute(tail, "dom", to_next)
    head = lax.ppermute(head, "dom", to_prev)

    return pl.pallas_call(
        functools.partial(back_kernel, dom_shift, sent, paired, rest > 0),
        grid=(grids,),
        in_specs=[SMEM] * 3 + [VMEM, VMEM] + [ANY] * (len(flat) + len(own)),
        out_specs=per_grid((other, block_len)),
        out_shape=jax.ShapeDtypeStruct((grids, other, block_len), f32),
        scratch_shapes=[
            pltpu.VMEM((sent * chunk + rest, other), f32),
            pltpu.VMEM((block_len + 2 * LINE, other), f32),
            pltpu.VMEM((block_len, other), f32),
            pltpu.SemaphoreType.DMA((sent + 1,)),
        ],
        compiler_params=pltpu.CompilerParams(vmem_limit_bytes=VMEM_BYTES),
        name="back",
    )(levels, velocity, starts, tail, head, *flat, *own)


def local(nodal_values, source_term, velocity, react_rate, levels, comb_coefs):
    grids, other, block_len = nodal_values.shape
    dom = lax.axis_size("dom")
    count = lax.axis_size("grid")
    dom_shift = dom.bit_length() - 1
    coarse = BASE // dom
    f32 = jnp.float32
    all_levels = [levels] + [lax.ppermute(levels, "grid", [(i, (i + k) % count) for i in range(count)]) for k in range(1, count)]

    values, first, last = pl.pallas_call(
        functools.partial(front_kernel, dom_shift),
        grid=(grids,),
        in_specs=[SMEM, SMEM, SMEM, per_grid((other, block_len)), per_grid((other, block_len))],
        out_specs=[per_grid((block_len, other)), per_grid((LINE, other)), per_grid((LINE, other))],
        out_shape=[
            jax.ShapeDtypeStruct((grids, block_len, other), f32),
            jax.ShapeDtypeStruct((grids, LINE, other), f32),
            jax.ShapeDtypeStruct((grids, LINE, other), f32),
        ],
        compiler_params=pltpu.CompilerParams(vmem_limit_bytes=VMEM_MOST),
        name="front",
    )(levels, velocity, react_rate, nodal_values, source_term)

    table = branch_table(coarse)
    starts, which = pl.pallas_call(
        functools.partial(plan_kernel, coarse, table),
        in_specs=[ANY] * count,
        out_specs=[SMEM, SMEM],
        scratch_shapes=[pltpu.SMEM(levels.shape, jnp.int32)] * count + [pltpu.SemaphoreType.DMA((count,))],
        out_shape=[jax.ShapeDtypeStruct((2 * len(GROUPS) + 2,), jnp.int32), jax.ShapeDtypeStruct((1,), jnp.int32)],
        name="plan",
    )(*all_levels)

    operands = (levels, velocity, comb_coefs, starts, values, first, last)
    branches = [functools.partial(run_branch, dom, *row) for row in table]
    return lax.switch(which[0], branches, operands)


def solution(mesh):
    in_specs = (
        P("grid", None, "dom"),
        P("grid", None, "dom"),
        P("grid", None),
        P("grid"),
        P("grid", None),
        P("grid"),
    )
    return jax.shard_map(local, mesh=mesh, in_specs=in_specs, out_specs=P("grid", None, "dom"), check_vma=False)
```

```python
import functools
import itertools

import jax
import jax.numpy as jnp
from jax import lax
from jax.experimental import pallas as pl
from jax.experimental.pallas import tpu as pltpu
from jax.sharding import PartitionSpec as P

MAXL = 8
MINL = 5
LSUM = 13
LINE = 2**MAXL
BASE = 2**MINL
TAU = 0.25
VMEM_BYTES = 48 * 2**20
VMEM_MOST = 63 * 2**20
BRANCHES = [(6, 3), (7, 4), (8, 4), (10, 5), (11, 4), (12, 4), (14, 5)]
AHEAD = 3
EARLY = 1

GROUPS = [(b, y) for b in range(MINL, MAXL + 1) for y in range(MINL, LSUM - b + 1)]
BAND_UNITS = [1] + [2**t for t in range(MAXL - MINL)]
BAND_FIRST = [0] + [2**t for t in range(MAXL - MINL)]


def group_rows(y):
    return 1 if y == MINL else 2 ** (y - MINL - 1)


GROUP_UNITS = [group_rows(y) * BAND_UNITS[b - MINL] for b, y in GROUPS]
TOTAL_UNITS = sum(GROUP_UNITS)
HEAD_GROUPS = [k for k, (b, y) in enumerate(GROUPS) if y == MINL]


def rows_at(unit, count=1):
    return pl.ds(pl.multiple_of(unit * BASE, BASE), count * BASE)


def region_units(y, coarse):
    rows = group_rows(y) * coarse
    return max(rows - 2, 0), min(rows, 2)


def group_sizes(coarse):
    inner, edge = zip(*[region_units(y, coarse) for _, y in GROUPS])
    widths = [BAND_UNITS[b - MINL] for b, _ in GROUPS]
    return [n * w for n, w in zip(inner, widths)], [n * w for n, w in zip(edge, widths)]


def branch_table(coarse):
    inner, edge = group_sizes(coarse)
    tops = [[-1] + list(range(MINL, LSUM - b + 1)) for b in range(MINL, MAXL + 1)]
    cases = []
    for top in itertools.product(*tops):
        if all(hi >= lo for hi, lo in zip(top, top[1:])):
            held = [y <= top[b - MINL] for b, y in GROUPS]
            cases.append((sum(n for n, h in zip(inner, held) if h), sum(n for n, h in zip(edge, held) if h)))
    table, low = [], -1
    for size, count in BRANCHES + [(TOTAL_UNITS, 5)]:
        chunk = -(-size * coarse // count)
        top = count * chunk
        fits = [(i, e) for i, e in cases if low < i + e <= top]
        if fits:
            before = min(min(i for i, _ in fits) // chunk, EARLY)
            spill = any(top > sum(inner) + e and e < sum(edge) for _, e in fits)
            end = count if spill else before - (-max(e for _, e in fits) // chunk)
            table.append((count, chunk, before, end))
            low = top
    return table


def plan_kernel(coarse, table, *refs):
    parts = (len(refs) - 3) // 2
    lev_refs, (start_ref, which_ref), (*held, sems) = refs[:parts], refs[parts : parts + 2], refs[parts + 2 :]
    loads = [pltpu.make_async_copy(src, dst, sems.at[n]) for n, (src, dst) in enumerate(zip(lev_refs, held))]
    for load in loads:
        load.start()
    for load in loads:
        load.wait()
    lev_refs = held
    shared = []
    for b, y in GROUPS:
        holders = jnp.int32(0)
        for lev_ref in lev_refs:
            held = jnp.int32(0)
            for c in range(lev_ref.shape[0]):
                held = held | jnp.where((lev_ref[c, 0] >= b) & (lev_ref[c, 1] >= y), 1, 0)
            holders = holders + held
        shared.append(jnp.where(holders >= 2, 1, 0))
    sizes = group_sizes(coarse)
    counts, starts = [], []
    for part in sizes:
        count = jnp.int32(0)
        places = [jnp.int32(0)] * len(GROUPS)
        for wanted in (1, 0):
            for k, size in enumerate(part):
                take = shared[k] == wanted
                places[k] = jnp.where(take, count, places[k])
                count = count + jnp.where(take, size, 0)
            if wanted:
                counts.append(count)
        starts.append(places)
    total = counts[0] + counts[1]
    which = jnp.int32(0)
    ahead = jnp.int32(table[0][2] * table[0][1])
    for (count, size, _, _), (_, later, before, _) in zip(table, table[1:]):
        more = total > count * size
        which = which + jnp.where(more, 1, 0)
        ahead = jnp.where(more, before * later, ahead)
    which_ref[0] = which
    for k in range(len(GROUPS)):
        start_ref[k] = starts[0][k]
        start_ref[len(GROUPS) + k] = starts[1][k] + jnp.where(shared[k] == 1, ahead, sum(sizes[0]))
    start_ref[2 * len(GROUPS)] = ahead
    start_ref[2 * len(GROUPS) + 1] = counts[1]


def inner_slot(start_ref, group, offset):
    place = start_ref[group] + offset
    return place + jnp.where(place >= start_ref[2 * len(GROUPS)], start_ref[2 * len(GROUPS) + 1], 0)


def point_of(index, points):
    tier = jnp.where(index >= 4 * BASE, 4 * BASE, jnp.where(index >= 2 * BASE, 2 * BASE, BASE))
    step = jnp.where(index >= 4 * BASE, points >> 8, jnp.where(index >= 2 * BASE, points >> 7, points >> 6))
    fine = index >= BASE
    place = jnp.where(fine, (2 * (index - tier) + 1) * step, index * (points >> MINL))
    return place, jnp.where(fine, step, 0), fine


def halves(x):
    high = x.astype(jnp.bfloat16)
    return high, (x - high.astype(jnp.float32)).astype(jnp.bfloat16)


def dot(a, b, dims):
    return lax.dot_general(a, b, dims, preferred_element_type=jnp.float32)


def front_kernel(dom_shift, lev_ref, vel_ref, rate_ref, v_ref, s_ref, u_ref, first_ref, last_ref):
    g = pl.program_id(0)
    lx = lev_ref[g, 0]
    points = jnp.int32(1) << lx
    live = jnp.int32(1) << (lx + lev_ref[g, 1] - dom_shift)
    nu = vel_ref[g, 0] * points.astype(jnp.float32) / LINE
    centre = 1.0 - nu * nu
    ahead = 0.5 * nu * nu - 0.5 * nu
    behind = 0.5 * nu * nu + 0.5 * nu
    damp = 1.0 - TAU * rate_ref[g]
    p = lax.broadcasted_iota(jnp.int32, (LINE, LINE), 0)
    q = lax.broadcasted_iota(jnp.int32, (LINE, LINE), 1)
    wrap = points - 1
    place, step, fine = point_of(p & wrap, points)
    same = (p >> lx) == (q >> lx)
    off = ((q & wrap) - place) & wrap
    lower = (off + step) & wrap
    upper = (off - step) & wrap
    half = jnp.where(fine, -0.5, 0.0)

    def adv(d):
        return jnp.where(d == 0, centre, jnp.where(d == 1, ahead, jnp.where(d == wrap, behind, 0.0)))

    def one(d):
        return jnp.where(d == 0, 1.0, 0.0)

    mat_v = jnp.where(same, damp * (adv(off) + half * (adv(lower) + adv(upper))), 0.0)
    mat_hi, mat_lo = halves(mat_v)
    mat_s = jnp.where(same, TAU * (one(off) + half * (one(lower) + one(upper))), 0.0).astype(jnp.bfloat16)
    nt = (((1,), (1,)), ((), ()))
    last_block = jnp.maximum(live // LINE - 1, 0)

    def one_block(block, _):
        cut = pl.ds(pl.multiple_of(block * LINE, LINE), LINE)
        v_hi, v_lo = halves(v_ref[0, :, cut])
        s_hi, s_lo = halves(s_ref[0, :, cut])
        res = dot(mat_hi, v_hi, nt) + dot(mat_lo, v_hi, nt) + dot(mat_hi, v_lo, nt) + dot(mat_s, s_hi, nt) + dot(mat_s, s_lo, nt)
        u_ref[0, cut, :] = res

        @pl.when(block == 0)
        def _():
            first_ref[0] = res

        @pl.when(block == last_block)
        def _():
            last_ref[0] = res

        return 0

    lax.fori_loop(0, last_block + 1, one_block, 0)


def y_coefs(nu):
    return 1.0 - nu * nu, 0.5 * nu * nu - 0.5 * nu, 0.5 * nu * nu + 0.5 * nu


def group_of(tier, xu):
    band = jnp.where(xu >= 4, 3, jnp.where(xu >= 2, 2, xu))
    group = jnp.where(band == 0, tier, jnp.where(band == 1, 4 + tier, jnp.where(band == 2, 7 + tier, 9)))
    width = jnp.where(band >= 2, 1 << (band - 1), 1)
    return group, width, xu - jnp.where(band >= 2, width, band)


class Shape:
    def __init__(self, lev_ref, g, dom_shift):
        self.lx, self.ly = lev_ref[g, 0], lev_ref[g, 1]
        self.live = jnp.int32(1) << (self.lx + self.ly - dom_shift)
        self.units = self.live // BASE
        self.x_shift = self.lx - MINL
        self.nx = jnp.int32(1) << self.x_shift
        self.points = jnp.int32(1) << self.lx
        self.seg_shift = self.ly - MINL
        self.rows = self.units >> self.x_shift

    def tier(self, tier):
        step = jnp.int32(1) << (self.seg_shift - tier)
        fine = tier > 0
        count = jnp.where(fine, self.rows >> (self.seg_shift - tier + 1), self.rows >> self.seg_shift)
        return count, jnp.where(fine, step, 0), jnp.where(fine, step, 0), jnp.where(fine, 2 * step, step)


def add_surplus(t_ref, mov, shape, step, places, weight):
    away = step << shape.x_shift
    half = jnp.where(step > 0, 0.5, 0.0)
    sums = []
    for y, xu, slot in places:
        i = (y << shape.x_shift) + xu
        value = mov[rows_at(i), :] - half * (mov[rows_at(i - away), :] + mov[rows_at(i + away), :])
        sums.append(t_ref[rows_at(slot), :] + weight * value)
    for (_, _, slot), value in zip(places, sums):
        t_ref[rows_at(slot), :] = value


def clear(t_ref):
    def one(i, _):
        t_ref[rows_at(i), :] = jnp.zeros((BASE, t_ref.shape[1]), jnp.float32)
        return 0

    lax.fori_loop(0, t_ref.shape[0] // BASE, one, 0)


def send_out(t_ref, out_refs, sems):
    moves, at = [], 0
    for n, out_ref in enumerate(out_refs):
        size = out_ref.shape[0]
        moves.append(pltpu.make_async_copy(t_ref.at[at : at + size, :], out_ref, sems.at[n]))
        at += size
    for move in moves:
        move.start()
    for move in moves:
        move.wait()


def inner_kernel(dom_shift, n_out, lev_ref, vel_ref, coef_ref, start_ref, u_ref, *refs):
    out_refs, (t_ref, mov, sems) = refs[:n_out], refs[n_out:]
    clear(t_ref)

    def one_grid(g, _):
        shape = Shape(lev_ref, g, dom_shift)
        nx, x_shift = shape.nx, shape.x_shift
        centre, ahead, behind = y_coefs(vel_ref[g, 1] * (jnp.int32(1) << shape.ly).astype(jnp.float32) / LINE)
        weight = coef_ref[g].astype(jnp.float32)

        def step_y(n, _):
            i = nx + 2 * n
            mov[rows_at(i, 2), :] = (
                centre * u_ref[g, rows_at(i, 2), :] + ahead * u_ref[g, rows_at(i + nx, 2), :] + behind * u_ref[g, rows_at(i - nx, 2), :]
            )
            return 0

        lax.fori_loop(0, jnp.maximum(shape.units - 2 * nx, 0) >> 1, step_y, 0)

        def tier_loop(tier, _):
            count, step, first, stride = shape.tier(tier)

            def two(pair, _):
                places = []
                for n in (2 * pair, 2 * pair + 1):
                    j, xu = (n >> x_shift) + 1, n & (nx - 1)
                    group, width, place = group_of(tier, xu)
                    places.append((first + j * stride, xu, inner_slot(start_ref, group, (j - 1) * width + place)))
                add_surplus(t_ref, mov, shape, step, places, weight)
                return 0

            lax.fori_loop(0, (jnp.maximum(count - 2, 0) << x_shift) >> 1, two, 0)
            return 0

        lax.fori_loop(0, shape.seg_shift + 1, tier_loop, 0)
        return 0

    lax.fori_loop(0, u_ref.shape[0], one_grid, 0)
    send_out(t_ref, out_refs, sems)


def edge_kernel(dom_shift, n_out, sent, lev_ref, vel_ref, coef_ref, start_ref, u_ref, rest_ref, next_ref, prev_ref, *refs):
    out_refs, (t_ref, mov, sems) = refs[:n_out], refs[n_out:]
    load = pltpu.make_async_copy(rest_ref, t_ref, sems.at[n_out])
    load.start()
    halo_units = next_ref.shape[1] // BASE
    at_once = min(2, BASE >> dom_shift)

    def one_grid(g, _):
        shape = Shape(lev_ref, g, dom_shift)
        nx, x_shift, units, rows = shape.nx, shape.x_shift, shape.units, shape.rows
        centre, ahead, behind = y_coefs(vel_ref[g, 1] * (jnp.int32(1) << shape.ly).astype(jnp.float32) / LINE)
        weight = coef_ref[g].astype(jnp.float32)
        prev_first = jnp.where(shape.live < LINE, units, halo_units) - nx

        def ends(xu, _):
            before = prev_ref[g, rows_at(prev_first + xu), :]
            head = u_ref[g, rows_at(xu), :]
            last = u_ref[g, rows_at(units - nx + xu), :]
            after = next_ref[g, rows_at(xu), :]

            @pl.when(rows == 1)
            def _():
                mov[rows_at(xu), :] = centre * head + ahead * after + behind * before

            @pl.when(rows > 1)
            def _():
                mov[rows_at(xu), :] = centre * head + ahead * u_ref[g, rows_at(nx + xu), :] + behind * before
                mov[rows_at(units - nx + xu), :] = centre * last + ahead * after + behind * u_ref[g, rows_at(units - 2 * nx + xu), :]

            @pl.when(shape.seg_shift > 0)
            def _():
                mov[rows_at(units + xu), :] = centre * after + ahead * next_ref[g, rows_at(nx + xu), :] + behind * last

            return 0

        lax.fori_loop(0, nx, ends, 0)

        def step_y(i, _):
            mov[rows_at(i), :] = centre * u_ref[g, rows_at(i), :] + ahead * u_ref[g, rows_at(i + nx), :] + behind * u_ref[g, rows_at(i - nx), :]
            return 0

        segment = jnp.int32(1) << shape.seg_shift
        near = jnp.minimum(segment, rows - 2)
        lax.fori_loop(nx, (near + 1) << x_shift, step_y, 0)
        lax.fori_loop(jnp.maximum(rows - segment, near + 1) << x_shift, (rows - 1) << x_shift, step_y, 0)

        @pl.when(g == 0)
        def _():
            load.wait()

        def tier_loop(tier, _):
            count, step, first, stride = shape.tier(tier)

            def several(batch, _):
                places = []
                for n in [batch * at_once + k for k in range(at_once)]:
                    end, xu = n >> x_shift, n & (nx - 1)
                    group, width, place = group_of(tier, xu)
                    slot = start_ref[len(GROUPS) + group] + end * width + place - sent
                    places.append((first + end * (count - 1) * stride, xu, slot))
                add_surplus(t_ref, mov, shape, step, places, weight)
                return 0

            lax.fori_loop(0, (jnp.minimum(count, 2) << x_shift) // at_once, several, 0)
            return 0

        lax.fori_loop(0, shape.seg_shift + 1, tier_loop, 0)
        return 0

    lax.fori_loop(0, u_ref.shape[0], one_grid, 0)
    send_out(t_ref, out_refs, sems)


def load_sums(t_ref, got, rest_ref, sems, first=0):
    count = lax.axis_size("grid")
    z = lax.axis_index("grid")
    passed_on = (z == 0) | (z == count - 1)
    at = 0
    waits = []
    for n, (total, passed) in enumerate(got):
        size = total.shape[0]
        dst = t_ref.at[at : at + size, :]
        if passed is None:
            pltpu.make_async_copy(total, dst, sems.at[n]).start()
        else:
            @pl.when(passed_on)
            def _():
                pltpu.make_async_copy(passed, dst, sems.at[n]).start()

            @pl.when(jnp.logical_not(passed_on))
            def _():
                pltpu.make_async_copy(total, dst, sems.at[n]).start()
        waits.append(pltpu.make_async_copy(total, dst, sems.at[n]))
        at += size
    if rest_ref is not None:
        at = t_ref.shape[0] - rest_ref.shape[0]
        waits.append(pltpu.make_async_copy(rest_ref, t_ref.at[at:, :], sems.at[len(got)]))
        waits[-1].start()
    for wait in waits:
        wait.wait()


def pairs_of(refs, count, paired):
    if paired:
        return [(refs[2 * n], refs[2 * n + 1]) for n in range(count)], refs[2 * count :]
    return [(refs[n], None) for n in range(count)], refs[count:]


def pack_kernel(coarse, sent, count, paired, has_rest, start_ref, *refs):
    got, refs = pairs_of(refs, count, paired)
    rest_ref, refs = (refs[0], refs[1:]) if has_rest else (None, refs)
    tail_ref, head_ref, t_ref, sems = refs
    load_sums(t_ref, got, rest_ref, sems)
    at = 0
    for k, (b, y) in enumerate(GROUPS):
        width = BAND_UNITS[b - MINL]
        last = start_ref[len(GROUPS) + k] + (region_units(y, coarse)[1] - 1) * width - sent
        tail_ref[at * BASE : (at + width) * BASE, :] = t_ref[rows_at(last, width), :]
        at += width
    at = 0
    for k in HEAD_GROUPS:
        width = BAND_UNITS[GROUPS[k][0] - MINL]
        head_ref[at * BASE : (at + width) * BASE, :] = t_ref[rows_at(start_ref[len(GROUPS) + k] - sent, width), :]
        at += width


def back_kernel(dom_shift, count, paired, has_rest, lev_ref, vel_ref, start_ref, tail_ref, head_ref, *refs):
    got, refs = pairs_of(refs, count, paired)
    rest_ref, refs = (refs[0], refs[1:]) if has_rest else (None, refs)
    out_ref, t_ref, val, comb, sems = refs
    g = pl.program_id(0)

    @pl.when(g == 0)
    def _():
        load_sums(t_ref, got, rest_ref, sems)

    shape = Shape(lev_ref, g, dom_shift)
    nx, x_shift, units, points, live, seg_shift, lx = shape.nx, shape.x_shift, shape.units, shape.points, shape.live, shape.seg_shift, shape.lx
    centre, ahead, behind = y_coefs(vel_ref[g, 1] * (jnp.int32(1) << shape.ly).astype(jnp.float32) / LINE)

    at_once = min(4, BASE >> dom_shift)

    def gather_tier(tier, _):
        rows, step, first, stride = shape.tier(tier)

        def several(batch, _):
            moves = []
            for n in [batch * at_once + k for k in range(at_once)]:
                j, xu = n >> x_shift, n & (nx - 1)
                group, width, place = group_of(tier, xu)
                inside = inner_slot(start_ref, group, (j - 1) * width + place)
                outside = start_ref[len(GROUPS) + group] + jnp.where(j > 0, width, 0) + place
                slot = jnp.where((j > 0) & (j < rows - 1), inside, outside)
                moves.append((nx + ((first + j * stride) << x_shift) + xu, t_ref[rows_at(slot), :]))
            for i, row in moves:
                val[rows_at(i), :] = row
            return 0

        lax.fori_loop(0, (rows << x_shift) // at_once, several, 0)
        return 0

    lax.fori_loop(0, seg_shift + 1, gather_tier, 0)

    def edges(xu, _):
        after = val[rows_at(nx + xu), :]
        band = jnp.where(xu >= 4, 3, jnp.where(xu >= 2, 2, xu))
        width = jnp.where(band >= 2, 1 << (band - 1), 1)
        base = jnp.where(band == 0, 0, jnp.where(band == 1, 4 + xu - 1, jnp.where(band == 2, 7 + xu - 2, 11 + xu - 4)))

        def finer(tier, row):
            return tail_ref[rows_at(base + tier * width), :] + 0.5 * (row + after)

        val[rows_at(xu), :] = lax.fori_loop(1, seg_shift + 1, finer, tail_ref[rows_at(base), :])
        val[rows_at(nx + units + xu), :] = head_ref[rows_at(xu), :]
        return 0

    lax.fori_loop(0, nx, edges, 0)

    def tier_loop(tier, _):
        step_shift = seg_shift - tier
        away = jnp.int32(1) << (step_shift + x_shift)

        def lift(batch, _):
            lifted = []
            for j in [batch * at_once + k for k in range(at_once)]:
                y = ((j >> x_shift) * 2 + 1) << step_shift
                i = nx + (y << x_shift) + (j & (nx - 1))
                lifted.append((i, val[rows_at(i), :] + 0.5 * (val[rows_at(i - away), :] + val[rows_at(i + away), :])))
            for i, row in lifted:
                val[rows_at(i), :] = row
            return 0

        lax.fori_loop(0, (units >> (step_shift + 1)) // at_once, lift, 0)
        return 0

    lax.fori_loop(1, seg_shift + 1, tier_loop, 0)

    def step_y(i, _):
        i = 4 * i
        comb[rows_at(i, 4), :] = centre * val[rows_at(i + nx, 4), :] + ahead * val[rows_at(i + 2 * nx, 4), :] + behind * val[rows_at(i, 4), :]
        return 0

    lax.fori_loop(0, units >> 2, step_y, 0)

    def clear(i, _):
        comb[rows_at(i), :] = jnp.zeros((BASE, comb.shape[1]), jnp.float32)
        return 0

    lax.fori_loop(units, comb.shape[0] // BASE, clear, 0)

    p = lax.broadcasted_iota(jnp.int32, (LINE, LINE), 0)
    q = lax.broadcasted_iota(jnp.int32, (LINE, LINE), 1)
    wrap = points - 1
    place, step, fine = point_of(p & wrap, points)
    reach = jnp.where(fine, step, points >> MINL)
    inverse = jnp.where(fine, jnp.where(reach == 4, 0.25, jnp.where(reach == 2, 0.5, 1.0)), 1.0 / (points >> MINL).astype(jnp.float32))
    off = ((q & wrap) - place) & wrap
    apart = jnp.minimum(off, points - off)
    hat = jnp.maximum(0.0, 1.0 - apart.astype(jnp.float32) * inverse)
    mat = jnp.where((p >> lx) == (q >> lx), hat, 0.0)
    mat = mat.astype(jnp.bfloat16)
    tn = (((0,), (0,)), ((), ()))
    live_blocks = jnp.maximum(live // LINE, 1)

    def one_block(block, _):
        cut = pl.ds(pl.multiple_of(block * LINE, LINE), LINE)
        high, low = halves(comb[cut, :])
        out_ref[0, :, cut] = dot(high, mat, tn) + dot(low, mat, tn)
        return 0

    def no_block(block, _):
        out_ref[0, :, pl.ds(pl.multiple_of(block * LINE, LINE), LINE)] = jnp.zeros((out_ref.shape[1], LINE), jnp.float32)
        return 0

    lax.fori_loop(0, live_blocks, one_block, 0)
    lax.fori_loop(live_blocks, out_ref.shape[2] // LINE, no_block, 0)


def sum_line(parts):
    count = lax.axis_size("grid")
    if count == 1:
        return [(part, None) for part in parts]
    if count % 2:
        return [(lax.psum(part, "grid"), None) for part in parts]
    half = count // 2
    z = lax.axis_index("grid")
    at_end = (z == 0) | (z == count - 1)
    inwards = [(0, 1), (count - 1, count - 2)]
    outwards = [(1, 0), (count - 2, count - 1)]
    number = len(parts)
    arrived, held, crossed, done = {}, {}, {}, {}
    if half > 1:
        arrived = {n: lax.ppermute(parts[n], "grid", inwards) for n in range(min(AHEAD, number))}

    def finish(n):
        total = held[n] + crossed[n]
        for i in range(half - 2, 0, -1):
            came = lax.ppermute(total, "grid", [(i + 1, i), (count - 2 - i, count - 1 - i)])
            total = jnp.where((z == i) | (z == count - 1 - i), came, total)
        if half == 1:
            done[n] = (total, None)
        elif n + AHEAD < number:
            arrived[n + AHEAD] = lax.ppermute(jnp.where(at_end, parts[n + AHEAD], total), "grid", inwards + outwards)
            done[n] = (total, arrived[n + AHEAD])
        else:
            done[n] = (total, lax.ppermute(total, "grid", outwards))

    for n in range(number):
        total = parts[n]
        if half > 1:
            if n:
                arrived[n], held[n - 1] = lax.optimization_barrier((arrived[n], held[n - 1]))
            total = total + arrived[n]
        for i in range(1, half - 1):
            total = total + lax.ppermute(total, "grid", [(i, i + 1), (count - 1 - i, count - 2 - i)])
        held[n] = total
        crossed[n] = lax.ppermute(total, "grid", [(half - 1, half), (half, half - 1)])
        if n:
            crossed[n - 1], held[n] = lax.optimization_barrier((crossed[n - 1], held[n]))
            finish(n - 1)
    finish(number - 1)
    return [done[n] for n in range(number)]


SMEM = pl.BlockSpec(memory_space=pltpu.SMEM)
VMEM = pl.BlockSpec(memory_space=pltpu.VMEM)
ANY = pl.BlockSpec(memory_space=pl.ANY)


def per_grid(shape):
    return pl.BlockSpec((1,) + shape, lambda g: (g, 0, 0))


def run_branch(dom, sent, size, inner, end, operands):
    levels, velocity, comb_coefs, starts, values, first, last = operands
    f32 = jnp.float32
    grids, block_len, other = values.shape
    dom_shift = dom.bit_length() - 1
    coarse = BASE // dom
    chunk = size * BASE
    rest = TOTAL_UNITS * coarse * BASE - sent * chunk
    later = sent - inner
    params = pltpu.CompilerParams(vmem_limit_bytes=VMEM_BYTES)
    to_next = [(i, (i + 1) % dom) for i in range(dom)]
    to_prev = [(i, (i - 1) % dom) for i in range(dom)]

    def rows(n):
        return jax.ShapeDtypeStruct((n, other), f32)

    after = lax.ppermute(first, "dom", to_prev)
    before = lax.ppermute(last, "dom", to_next)

    outs = [rows(chunk)] * inner + [rows(later * chunk + rest)]
    *parts, held = pl.pallas_call(
        functools.partial(inner_kernel, dom_shift, len(outs)),
        in_specs=[SMEM] * 4 + [VMEM],
        out_specs=[ANY] * len(outs),
        out_shape=outs,
        scratch_shapes=[
            pltpu.VMEM((TOTAL_UNITS * coarse * BASE, other), f32),
            pltpu.VMEM((block_len + LINE, other), f32),
            pltpu.SemaphoreType.DMA((len(outs),)),
        ],
        compiler_params=params,
        name="inner",
    )(levels, velocity, comb_coefs, starts, values)

    outs = [rows(chunk)] * later + [rows(rest)] * (rest > 0)
    edges = list(pl.pallas_call(
        functools.partial(edge_kernel, dom_shift, len(outs), inner * chunk // BASE),
        in_specs=[SMEM] * 4 + [VMEM, ANY, VMEM, VMEM],
        out_specs=[ANY] * len(outs),
        out_shape=outs,
        scratch_shapes=[
            pltpu.VMEM((later * chunk + rest, other), f32),
            pltpu.VMEM((block_len + LINE, other), f32),
            pltpu.SemaphoreType.DMA((len(outs) + 1,)),
        ],
        compiler_params=params,
        name="edge",
    )(levels, velocity, comb_coefs, starts, values, held, after, before))
    own = edges[later:]
    parts = parts + edges[:later]

    summed = sum_line(parts)
    paired = summed[0][1] is not None
    flat = [x for n in range(sent) for x in summed[n] if x is not None]
    flat_later = [x for n in range(inner, end) for x in summed[n] if x is not None]

    tail_rows = sum(BAND_UNITS[b - MINL] for b, _ in GROUPS) * BASE
    head_rows = sum(BAND_UNITS) * BASE
    tail, head = pl.pallas_call(
        functools.partial(pack_kernel, coarse, inner * size, end - inner, paired, rest > 0),
        in_specs=[SMEM] + [ANY] * (len(flat_later) + len(own)),
        out_specs=[VMEM, VMEM],
        out_shape=[rows(tail_rows), rows(head_rows)],
        scratch_shapes=[pltpu.VMEM((later * chunk + rest, other), f32), pltpu.SemaphoreType.DMA((end - inner + 1,))],
        compiler_params=params,
        name="pack",
    )(starts, *flat_later, *own)
    tail = lax.ppermute(tail, "dom", to_next)
    head = lax.ppermute(head, "dom", to_prev)

    return pl.pallas_call(
        functools.partial(back_kernel, dom_shift, sent, paired, rest > 0),
        grid=(grids,),
        in_specs=[SMEM] * 3 + [VMEM, VMEM] + [ANY] * (len(flat) + len(own)),
        out_specs=per_grid((other, block_len)),
        out_shape=jax.ShapeDtypeStruct((grids, other, block_len), f32),
        scratch_shapes=[
            pltpu.VMEM((sent * chunk + rest, other), f32),
            pltpu.VMEM((block_len + 2 * LINE, other), f32),
            pltpu.VMEM((block_len, other), f32),
            pltpu.SemaphoreType.DMA((sent + 1,)),
        ],
        compiler_params=pltpu.CompilerParams(vmem_limit_bytes=VMEM_BYTES),
        name="back",
    )(levels, velocity, starts, tail, head, *flat, *own)


def local(nodal_values, source_term, velocity, react_rate, levels, comb_coefs):
    grids, other, block_len = nodal_values.shape
    dom = lax.axis_size("dom")
    count = lax.axis_size("grid")
    dom_shift = dom.bit_length() - 1
    coarse = BASE // dom
    f32 = jnp.float32
    all_levels = [levels] + [lax.ppermute(levels, "grid", [(i, (i + k) % count) for i in range(count)]) for k in range(1, count)]

    values, first, last = pl.pallas_call(
        functools.partial(front_kernel, dom_shift),
        grid=(grids,),
        in_specs=[SMEM, SMEM, SMEM, per_grid((other, block_len)), per_grid((other, block_len))],
        out_specs=[per_grid((block_len, other)), per_grid((LINE, other)), per_grid((LINE, other))],
        out_shape=[
            jax.ShapeDtypeStruct((grids, block_len, other), f32),
            jax.ShapeDtypeStruct((grids, LINE, other), f32),
            jax.ShapeDtypeStruct((grids, LINE, other), f32),
        ],
        compiler_params=pltpu.CompilerParams(vmem_limit_bytes=VMEM_MOST),
        name="front",
    )(levels, velocity, react_rate, nodal_values, source_term)

    table = branch_table(coarse)
    starts, which = pl.pallas_call(
        functools.partial(plan_kernel, coarse, table),
        in_specs=[ANY] * count,
        out_specs=[SMEM, SMEM],
        scratch_shapes=[pltpu.SMEM(levels.shape, jnp.int32)] * count + [pltpu.SemaphoreType.DMA((count,))],
        out_shape=[jax.ShapeDtypeStruct((2 * len(GROUPS) + 2,), jnp.int32), jax.ShapeDtypeStruct((1,), jnp.int32)],
        name="plan",
    )(*all_levels)

    operands = (levels, velocity, comb_coefs, starts, values, first, last)
    branches = [functools.partial(run_branch, dom, *row) for row in table]
    return lax.switch(which[0], branches, operands)


def solution(mesh):
    in_specs = (
        P("grid", None, "dom"),
        P("grid", None, "dom"),
        P("grid", None),
        P("grid"),
        P("grid", None),
        P("grid"),
    )
    return jax.shard_map(local, mesh=mesh, in_specs=in_specs, out_specs=P("grid", None, "dom"), check_vma=False)
```
